128 devices in a mesh: region: 64 (over z, y, x), chan: 2 (over core).
Axes of the slice: x: 4, y: 4, z: 4, core: 2. Of those that a mesh axis runs over, the one named last changes fastest.
Arguments:
- patches: bfloat16 [4096, 8192], P('region', 'chan'), may hold values from -6 to 6
- patch_region: int32 [4096, 2], P('region'), may hold values from 0 to 63, all different within a row; in each aligned block of 64 rows (0 to 63, 64 to 127, ...) at most 4 rows name the same one
- patch_cell: int32 [4096, 2], P('region'), may hold values from 0 to 31
- w_first: bfloat16 [9, 128, 64], P(None, 'chan'), may hold values from -0.25 to 0.25
- w_down: bfloat16 [9, 256, 128], P(None, 'chan'), may hold values from -0.1875 to 0.1875
- w_deep: bfloat16 [9, 256, 256], P(None, 'chan'), may hold values from -0.125 to 0.125
- w_merge: bfloat16 [9, 128, 384], replicated, may hold values from -0.109375 to 0.109375
- w_out: bfloat16 [9, 64, 128], replicated, may hold values from -0.1875 to 0.1875
Outputs:
- downscaled: bfloat16 [64, 2048, 128], P('chan', 'region')
The draws below stay inside these ranges and needn't reach their ends.
Inputs may be any that keep to these rules, and one draw needn't show every extreme that they name: `patch_region`: among the routes of the patches of one index of region, no region is named more than 4 times, a bound that some block reaches; a patch names 2 different regions.
All inputs are finite; a program needn't handle non-finite values.
Results may differ from the reference program's by a relative error of at most 0.013.
Values may be sent and summed in bfloat16 or wider, within the bound.
A program may use at most 64 MiB of HBM per device.

```python
import math
import jax
import jax.numpy as jnp
import numpy as np
from jax import lax

C0 = 64
C1 = 128
C2 = 256
TILE_H = 32
TILE_W = 128
PH = 8
PW = 16
PATCH_DEV = 64
TOP = 2
BLOCKS = 32
REGIONS = 64
PATCHES = 4096
MOST = 4


def with_ends(values, rng, smallest, largest):
    longest = values.shape.index(max(values.shape))
    spots = []
    for shift in (0, 1):
        where = [jax.random.randint(jax.random.fold_in(rng, axis), (), 0, length) for axis, length in enumerate(values.shape)]
        where[longest] = (where[longest] + shift) % values.shape[longest]
        spots.append(tuple(where))
    return values.at[spots[0]].set(smallest).at[spots[1]].set(largest)


def block_scale(own_key, extent, pieces, low, high):
    factor_of, own = 1.0, jax.random.fold_in(own_key, 6)
    for axis_at, shards_of in pieces:
        steps = jnp.exp(jax.random.uniform(jax.random.fold_in(own, axis_at), (shards_of,), jnp.float32, low / len(pieces), high / len(pieces)))
        factor_of = factor_of * jnp.repeat(steps, extent[axis_at] // shards_of).reshape([-1 if axis == axis_at else 1 for axis in range(len(extent))])
    return factor_of


def shared_out(rng, own, number, rows, number_of, top, bound, lean):
    order = jax.random.permutation(rng, number_of)
    crowded, usual = shares(number_of, rows * top, bound, lean, True), shares(number_of, rows * top, bound, lean, False)
    places = jnp.arange(number_of)

    def named(tallies, offset_by):
        used = int((tallies > 0).sum())
        fixed = max(1, used // 4)
        moved = fixed + (places - fixed + offset_by * (used - fixed)) % max(1, number_of - fixed)
        return jnp.zeros((number_of,), jnp.int32).at[order[jnp.where(places < fixed, places, moved)]].set(jnp.asarray(tallies, jnp.int32))

    tallies = jnp.where(number % 4 == 0, named(crowded, number // 4), named(usual, number - number // 4 - 1))
    mixed = jax.random.permutation(jax.random.fold_in(own, 3), number_of)
    giver, receiver = mixed[0:number_of // 2 * 2:2], mixed[1:number_of // 2 * 2:2]
    room = jnp.minimum(tallies[giver] - 1, bound - tallies[receiver]) // 2
    room = jnp.where((giver == order[0]) | (receiver == order[0]) | (tallies[receiver] == 0), 0, jnp.maximum(room, 0))
    moved = jax.random.randint(jax.random.fold_in(own, 4), (number_of // 2,), 0, 1 << 20) % (room + 1)
    tallies = tallies.at[giver].add(-moved).at[receiver].add(moved)
    items = jnp.searchsorted(jnp.cumsum(tallies), jnp.arange(rows * top), side="right").astype(jnp.int32)
    listing = items.reshape(top, rows).T
    listing = listing[jax.random.permutation(jax.random.fold_in(own, 1), rows)]
    offset_by = jax.random.randint(jax.random.fold_in(own, 2), (rows, 1), 0, top)
    return jnp.take_along_axis(listing, (jnp.arange(top)[None, :] + offset_by) % top, axis=1)


def shares(amount, total, most, lean, full):
    weights = [(1 << 20) // math.isqrt(standing ** lean) + 1 for standing in range(1, amount + 1)]
    largest = most if full else min(most, max(-(-total // amount), total * weights[0] // sum(weights)))
    least = 1 if total - largest >= amount - 1 else 0
    counts, spare = [largest] + [least] * (amount - 1), total - largest - least * (amount - 1)
    while spare > 0:
        movable = [i for i in range(1, amount) if counts[i] < largest] or [i for i in range(1, amount) if counts[i] < most]
        pool, budget = sum([weights[i] for i in movable]), spare
        for i in movable:
            addition = min(most - counts[i], max(1, budget * weights[i] // pool), spare)
            counts[i] = counts[i] + addition
            spare = spare - addition
    return np.array(counts)


def gaussian(own_key, shape, width, bound, pieces=(), dtype=jnp.bfloat16):
    level = block_scale(own_key, shape, pieces, -0.22, 0.18) if pieces else 1.0
    array = jax.random.normal(own_key, shape, jnp.float32) * width * level
    return jnp.minimum(jnp.maximum(array, -bound), bound).astype(dtype)


def setup_inputs(seed: int = 0) -> dict:
    key_list = jax.random.split(jax.random.key(seed), 9)
    patches = gaussian(key_list[0], (PATCHES, C0 * PH * PW), 1.0, 6.0, ((0, 64), (1, 2)))
    patch_region_keys = jax.random.split(jax.random.fold_in(key_list[1], 1), PATCHES // PATCH_DEV)
    patch_region_turns = jax.random.permutation(jax.random.fold_in(key_list[1], 3), PATCHES // PATCH_DEV)
    patch_region = jax.vmap(lambda own, number: shared_out(jax.random.fold_in(key_list[1], 2), own, number, PATCH_DEV, REGIONS, TOP, MOST, 2))(patch_region_keys, patch_region_turns).reshape((PATCHES, TOP))
    patch_cell = with_ends(jax.random.randint(key_list[2], (PATCHES, TOP), 0, BLOCKS), jax.random.fold_in(key_list[2], 1), 0, BLOCKS - 1).astype(jnp.int32)
    w_first = gaussian(key_list[3], (9, C1, C0), (9 * C0) ** -0.5, 0.25, ((1, 2),))
    w_down = gaussian(key_list[4], (9, C2, C1), (9 * C1) ** -0.5, 0.1875, ((1, 2),))
    w_deep = gaussian(key_list[5], (9, C2, C2), (9 * C2) ** -0.5, 0.125, ((1, 2),))
    w_merge = gaussian(key_list[6], (9, C1, C1 + C2), (9 * (C1 + C2)) ** -0.5, 0.109375)
    w_out = gaussian(key_list[7], (9, C0, C1), (9 * C1) ** -0.5, 0.1875)
    return {"patches": patches, "patch_region": patch_region, "patch_cell": patch_cell, "w_first": w_first, "w_down": w_down, "w_deep": w_deep, "w_merge": w_merge, "w_out": w_out}


def conv_taps(weights, padded_rows, stride, out_rows, out_cols):
    chans = padded_rows.shape[0]
    padded = jnp.pad(padded_rows, ((0, 0), (0, 0), (1, 1)))
    total = jnp.zeros((weights.shape[1], out_rows * out_cols), jnp.float32)
    for row_off in range(3):
        for col_off in range(3):
            window = lax.slice(padded, (0, row_off, col_off), (chans, row_off + stride * (out_rows - 1) + 1, col_off + stride * (out_cols - 1) + 1), (1, stride, stride))
            total = total + jnp.dot(weights[3 * row_off + col_off], window.reshape(chans, out_rows * out_cols), preferred_element_type=jnp.float32)
    return total.reshape(weights.shape[1], out_rows, out_cols)


def pad_rows(field):
    return jnp.pad(field, ((0, 0), (1, 1), (0, 0)))


def reference(patches, patch_region, patch_cell, w_first, w_down, w_deep, w_merge, w_out):
    routed = jnp.repeat(patches.astype(jnp.float32), TOP, axis=0)
    targets = (patch_region * BLOCKS + patch_cell).reshape(-1).astype(jnp.int32)
    summed = jax.ops.segment_sum(routed, targets, num_segments=REGIONS * BLOCKS).astype(jnp.bfloat16)
    grid = summed.reshape(REGIONS, TILE_H // PH, TILE_W // PW, C0, PH, PW).transpose(3, 0, 1, 4, 2, 5).reshape(C0, REGIONS * TILE_H, TILE_W)
    height = REGIONS * TILE_H
    first = jax.nn.silu(conv_taps(w_first, pad_rows(grid), 1, height, TILE_W)).astype(jnp.bfloat16)
    second = jax.nn.silu(conv_taps(w_down, pad_rows(first), 2, height // 2, TILE_W // 2)).astype(jnp.bfloat16)
    third = (jax.nn.silu(conv_taps(w_deep, pad_rows(second), 1, height // 2, TILE_W // 2)) + second.astype(jnp.float32)).astype(jnp.bfloat16)
    upsampled = jnp.repeat(jnp.repeat(third, 2, axis=1), 2, axis=2)
    joined = jnp.concatenate([first, upsampled], axis=0)
    fourth = jax.nn.silu(conv_taps(w_merge, pad_rows(joined), 1, height, TILE_W)).astype(jnp.bfloat16)
    result = grid.astype(jnp.float32) + conv_taps(w_out, pad_rows(fourth), 1, height, TILE_W)
    return result.astype(jnp.bfloat16)
```

```python
import jax
import jax.numpy as jnp
from jax import lax
from jax.experimental import pallas as pl
from jax.experimental.pallas import tpu as pltpu
from jax.sharding import PartitionSpec as P

C0 = 64
C1 = 128
C2 = 256
W = 128
HALF = 16
F32 = jnp.float32
BF16 = jnp.bfloat16
MESH = pl.DeviceIdType.MESH

OFFSETS = sorted(
    range(1, 64),
    key=lambda g: (-sum(min(v, 4 - v) for v in (g // 16, (g // 4) % 4, g % 4)), (g * 37) % 64),
)


def iota(shape, axis):
    return lax.broadcasted_iota(jnp.int32, shape, axis)


def shift(x, step):
    lane = iota(x.shape, 1)
    keep = lane < W - step if step > 0 else lane >= -step
    return jnp.where(keep, pltpu.roll(x, (-step) % W, 1), 0.0)


def silu(v):
    h = 0.5 * v
    return h + h * jnp.tanh(h)


def swap_granules(x):
    rows = x.shape[0]
    row, gran = iota(x.shape, 0), iota(x.shape, 1) // 16
    for s in (1, 2, 4):
        down = pltpu.roll(pltpu.roll(x, 16 * s, 1), rows - s, 0)
        up = pltpu.roll(pltpu.roll(x, W - 16 * s, 1), s, 0)
        row_bit, gran_bit = (row & s) != 0, (gran & s) != 0
        x = jnp.where(row_bit == gran_bit, x, jnp.where(gran_bit, down, up))
    return x


def kernel(
    patches_ref, region_ref, cell_ref, wf_ref, wd_ref, wp_ref, wm_ref, wo_ref,
    out_ref,
    payload, arrived, cells_out, cells_in,
    wf, wd, wp, wm, wo,
    place, grid_f, grid_own, grid, im1, im2, imd, im4, out_f, out_b,
    a2a_send, a2a_recv, cell_send, cell_recv, w_send, w_recv, g_send, g_recv, o_send, o_recv,
):
    r, c = lax.axis_index("region"), lax.axis_index("chan")
    mz, my, mx = r // 16, (r // 4) % 4, r % 4
    other = 1 - c

    def at_offset(g):
        return ((mz + g // 16) % 4) * 16 + ((my + (g // 4) % 4) % 4) * 4 + (mx + g % 4) % 4

    def remote(src, dst, send, recv, device):
        return pltpu.make_async_remote_copy(
            src_ref=src, dst_ref=dst, send_sem=send, recv_sem=recv,
            device_id=device, device_id_type=MESH,
        )

    def greet(device):
        pl.semaphore_signal(barrier, inc=1, device_id=device, device_id_type=MESH)

    barrier = pltpu.get_barrier_semaphore()
    for g in OFFSETS:
        greet((at_offset(g), c))
    greet((r, other))
    greet(((r + 63 + 2 * c) % 64, other))

    eye = iota((64, 64), 0) == iota((64, 64), 1)
    lower = (iota((64, 64), 1) < iota((64, 64), 0)).astype(F32).astype(BF16)
    hits, counts, starts = [], [], []
    before = jnp.zeros((1, 64), F32)
    for t in range(2):
        target = region_ref[:, t : t + 1]
        gz, gy, gx = (target // 16 - mz) & 3, ((target // 4) % 4 - my) & 3, (target % 4 - mx) & 3
        offset = gz * 16 + gy * 4 + gx
        hit = jnp.where(iota((64, 64), 1) == offset, 1.0, 0.0)
        count = jnp.dot(lower, hit.astype(BF16), preferred_element_type=F32) + before
        before = before + jnp.sum(hit, axis=0, keepdims=True)
        rank = jnp.sum(hit * count, axis=1, keepdims=True)
        hits.append(hit)
        counts.append(count)
        starts.append(offset.astype(F32) * 16.0 + rank)
    lane256 = iota((64, 256), 1)
    spread = iota((64, 256), 0) == lane256 % 64
    quarter = (4 * (iota((1, 256), 1) // 64)).astype(F32)
    rows_of = [
        jnp.sum(jnp.where(spread, s, 0.0), axis=0, keepdims=True) + quarter for s in starts
    ]
    stacked = jnp.concatenate([patches_ref[:, 1024 * q : 1024 * q + 1024] for q in range(4)], axis=0)
    for k in range(4):
        row = (iota((256, 256), 0) + 256 * k).astype(F32)
        chosen = jnp.where((row == rows_of[0]) | (row == rows_of[1]), 1.0, 0.0).astype(BF16)
        payload[16 * k : 16 * k + 16] = (
            jnp.dot(chosen, stacked, preferred_element_type=F32).astype(BF16).reshape(16, 16, 1024)
        )
    lane = iota((64, W), 1)
    codes = jnp.full((64, W), -1.0, F32)
    for k in range(4):
        value = jnp.zeros((1, 64), F32)
        for t in range(2):
            cell = cell_ref[:, t : t + 1].astype(F32) + 1.0
            value = value + jnp.sum(
                jnp.where(counts[t] == float(k), hits[t] * cell, 0.0), axis=0, keepdims=True
            )
        column = jnp.sum(jnp.where(eye, value, 0.0), axis=1, keepdims=True) - 1.0
        code = jnp.where(column >= 0.0, column + (32 * ((lane // 4) % 4)).astype(F32), -1.0)
        codes = jnp.where(lane % 4 == k, code, codes)
    cells_out[:, 0, :] = codes

    pl.semaphore_wait(barrier, 65)
    for g in OFFSETS:
        remote(cells_out.at[g], cells_in.at[g], cell_send, cell_recv, (at_offset(g), c)).start()
    for g in OFFSETS:
        remote(payload.at[g], arrived.at[g], a2a_send, a2a_recv, (at_offset(g), c)).start()
    arrived[0] = payload[0]
    cells_in[0] = cells_out[0]

    first_rows = pl.ds(pl.multiple_of(64 * c, 64), 64)
    second_rows = pl.ds(pl.multiple_of(128 * c, 128), 128)
    wf[first_rows, :] = jnp.concatenate([wf_ref[k] for k in range(9)], axis=1)
    for k in range(9):
        wd[second_rows, 128 * k : 128 * k + 128] = wd_ref[k]
        wp[second_rows, 256 * k : 256 * k + 256] = wp_ref[k]
    weight_copies = [
        remote(buf.at[rows], buf.at[rows], w_send.at[n], w_recv.at[n], (r, other))
        for n, (buf, rows) in enumerate([(wf, first_rows), (wd, second_rows), (wp, second_rows)])
    ]
    for copy in weight_copies:
        copy.start()
    for k in range(9):
        i, j = k // 3, k % 3
        wm[:, 1152 * i + 128 * j : 1152 * i + 128 * j + 128] = wm_ref[k, :, :C1]
        wm[:, 1152 * i + 384 + 256 * j : 1152 * i + 384 + 256 * j + 256] = wm_ref[k, :, C1:]
        wo[:, 128 * k : 128 * k + 128] = wo_ref[k]

    remote(
        cells_out.at[pl.ds(1, 63)], cells_in.at[pl.ds(1, 63)], cell_send, cell_recv, (r, other)
    ).wait_recv()
    owner = iota((8, W), 0) == iota((8, W), 1) // 16
    for b in range(8):
        code = jnp.sum(
            jnp.where(owner, cells_in[8 * b : 8 * b + 8, 0, :], 0.0), axis=0, keepdims=True
        )
        place[:, W * b : W * b + W] = jnp.where(
            iota((W, W), 0).astype(F32) == code, 1.0, 0.0
        ).astype(BF16)
    remote(
        payload.at[pl.ds(1, 63)], arrived.at[pl.ds(1, 63)], a2a_send, a2a_recv, (r, other)
    ).wait_recv()

    for n in range(4):
        sums = jnp.dot(
            place[...],
            arrived[:, :, 256 * n : 256 * n + 256].reshape(1024, 256),
            preferred_element_type=F32,
        )
        for h in range(2):
            block = swap_granules(sums[:, W * h : W * h + W])
            for q in range(4):
                for band in range(4):
                    at = 8 * (4 * q + band)
                    grid_f[pl.ds(256 * band + 8 * q + 2 * n + h, 8, stride=32), :] = block[at : at + 8]
    grid_own[...] = grid_f[...].astype(BF16).reshape(32, 32, W)

    own = pl.ds(pl.multiple_of(32 * c, 32), 32)
    grid_copies = [
        remote(
            grid_own.at[pl.ds(10 * other, 22)], grid.at[pl.ds(6 * c, 22), own],
            g_send.at[0], g_recv.at[2], (r, other),
        ),
        remote(
            grid_own.at[pl.ds(26, 6)], grid.at[pl.ds(0, 6), own],
            g_send.at[1], g_recv.at[c], ((r + 1) % 64, 0),
        ),
        remote(
            grid_own.at[pl.ds(0, 6)], grid.at[pl.ds(22, 6), own],
            g_send.at[2], g_recv.at[c], ((r + 63) % 64, 1),
        ),
    ]
    for copy in grid_copies:
        copy.start()
    grid[pl.ds(6 * other, 22), own, :] = grid_own[pl.ds(10 * c, 22)]
    grid_copies[0].wait_recv()
    for n in range(2):
        remote(
            grid_own.at[pl.ds(0, 6)], grid.at[pl.ds(0, 6), pl.ds(0, 32)],
            g_send.at[1], g_recv.at[n], (r, other),
        ).wait_recv()
    top = jnp.logical_and(r == 0, c == 0)
    bottom = jnp.logical_and(r == 63, c == 1)

    @pl.when(top)
    def _():
        grid[0:6] = jnp.zeros((6, C0, W), BF16)

    @pl.when(bottom)
    def _():
        grid[22:28] = jnp.zeros((6, C0, W), BF16)

    keep_top = jnp.where(top, 0.0, 1.0)
    keep_bottom = jnp.where(bottom, 0.0, 1.0)
    even = iota((C2, W), 1) % 2 == 0

    def cols(x):
        return jnp.concatenate([shift(x, -1), x, shift(x, 1)], axis=0)

    def widen(l, _):
        im1[l] = cols(grid[l].astype(F32)).astype(BF16)
        return 0

    lax.fori_loop(0, 28, widen, 0, unroll=4)
    for copy in weight_copies:
        copy.wait_recv()

    def first_rows_of(n, _):
        f = 4 * n
        window = jnp.concatenate(
            [im1[pl.ds(f + t, 3)].reshape(576, W) for t in range(4)], axis=1
        )
        total = jnp.dot(wf[...], window, preferred_element_type=F32)
        for t in range(4):
            factor = jnp.where(f + t < 5, keep_top, jnp.where(f + t >= 21, keep_bottom, 1.0))
            row = silu(total[:, W * t : W * t + W]) * factor
            im2[f + t, 0:384] = cols(row).astype(BF16)
        return 0

    lax.fori_loop(0, 7, first_rows_of, 0)

    def spread_pair(x):
        return jnp.concatenate([shift(x, -2), x, shift(x, 2)], axis=0).astype(BF16)

    pairs = []
    for m in range(6):
        window = jnp.concatenate(
            [
                jnp.concatenate([im2[4 * m + 2 * t + i, 0:384] for i in range(3)], axis=0)
                for t in range(2)
            ],
            axis=1,
        )
        total = jnp.dot(wd[...], window, preferred_element_type=F32)
        pair = silu(jnp.where(even, total[:, :W], pltpu.roll(total[:, W:], 1, 1)))
        if m == 0:
            pair = pair * keep_top
        if m == 5:
            pair = pair * keep_bottom
        pair = pair.astype(BF16).astype(F32)
        imd[2 * m] = spread_pair(pair)
    for m in range(5):
        a = imd[2 * m, C2 : 2 * C2].astype(F32)
        b = imd[2 * m + 2, C2 : 2 * C2].astype(F32)
        imd[2 * m + 1] = spread_pair(jnp.where(even, shift(a, 1), shift(b, -1)))

    for ms in ((0, 1), (2, 3), (4,)):
        window = jnp.concatenate([imd[2 * m : 2 * m + 3].reshape(2304, W) for m in ms], axis=1)
        total = jnp.dot(wp[...], window, preferred_element_type=F32)
        for t, m in enumerate(ms):
            third = silu(total[:, W * t : W * t + W]) + imd[2 * m + 1, C2 : 2 * C2].astype(F32)
            if m == 0:
                third = jnp.where(even, third * keep_top, third)
            if m == 4:
                third = jnp.where(even, third, third * keep_bottom)
            l1, l2, r1, r2 = shift(third, -1), shift(third, -2), shift(third, 1), shift(third, 2)
            edge = iota((C2, W), 1) < W - 1
            ups = (
                (
                    jnp.where(even, l2, l1),
                    jnp.where(even, third, l1),
                    jnp.where(edge, jnp.where(even, third, r1), 0.0),
                ),
                (
                    jnp.where(even, l1, third),
                    jnp.where(even, r1, third),
                    jnp.where(even, r1, r2),
                ),
            )
            for half in range(2):
                for j in range(3):
                    value = ups[half][j].astype(BF16)
                    if half == 0 and j == 0:
                        value = jnp.where(iota((C2, W), 1) == 0, 0.0, ups[half][j]).astype(BF16)
                    f = 4 * m + 3 + 2 * half
                    im2[f, 384 + C2 * j : 384 + C2 * j + C2] = value
                    im2[f + 1, 384 + C2 * j : 384 + C2 * j + C2] = value

    def fourth_rows(n, _):
        g = 2 * n
        window = jnp.concatenate(
            [im2[pl.ds(g + 3 + t, 3)].reshape(3456, W) for t in range(2)], axis=1
        )
        total = jnp.dot(wm[...], window, preferred_element_type=F32)
        for t in range(2):
            factor = jnp.where(g + t < 1, keep_top, jnp.where(g + t >= 17, keep_bottom, 1.0))
            im4[g + t] = cols(silu(total[:, W * t : W * t + W]) * factor).astype(BF16)
        return 0

    lax.fori_loop(0, 9, fourth_rows, 0)

    def out_rows(n, _):
        f = 4 * n
        window = jnp.concatenate(
            [im4[pl.ds(f + t, 3)].reshape(1152, W) for t in range(4)], axis=1
        )
        total = jnp.dot(wo[...], window, preferred_element_type=F32)
        for t in range(4):
            row = total[:, W * t : W * t + W] + grid[f + t + 6].astype(F32)
            out_f[pl.ds(f + t, C0, stride=HALF), :] = row
        return 0

    lax.fori_loop(0, 4, out_rows, 0)
    out_b[...] = out_f[...].astype(BF16).reshape(C0, HALF, W)
    mine = pl.ds(pl.multiple_of(HALF * c, HALF), HALF)
    out_copy = remote(
        out_b.at[pl.ds(32 * other, 32)], out_ref.at[:, mine, :], o_send, o_recv, (r, other)
    )
    out_copy.start()
    out_ref[:, mine, :] = out_b[pl.ds(32 * c, 32)]

    for copy in weight_copies + grid_copies:
        copy.wait_send()
    remote(
        cells_out.at[pl.ds(1, 63)], cells_in.at[pl.ds(1, 63)], cell_send, cell_recv, (r, other)
    ).wait_send()
    remote(
        payload.at[pl.ds(1, 63)], arrived.at[pl.ds(1, 63)], a2a_send, a2a_recv, (r, other)
    ).wait_send()
    out_copy.wait()


def shards(*args):
    vmem = pl.BlockSpec(memory_space=pltpu.VMEM)
    dma = pltpu.SemaphoreType.DMA
    return pl.pallas_call(
        kernel,
        out_shape=jax.ShapeDtypeStruct((32, 32, W), BF16),
        in_specs=[vmem] * 8,
        out_specs=vmem,
        scratch_shapes=[
            pltpu.VMEM((64, 16, 1024), BF16),
            pltpu.VMEM((64, 16, 1024), BF16),
            pltpu.VMEM((64, 1, W), F32),
            pltpu.VMEM((64, 1, W), F32),
            pltpu.VMEM((C1, 9 * C0), BF16),
            pltpu.VMEM((C2, 9 * C1), BF16),
            pltpu.VMEM((C2, 9 * C2), BF16),
            pltpu.VMEM((C1, 9 * (C1 + C2)), BF16),
            pltpu.VMEM((C0, 9 * C1), BF16),
            pltpu.VMEM((W, 1024), BF16),
            pltpu.VMEM((1024, W), F32),
            pltpu.VMEM((32, 32, W), BF16),
            pltpu.VMEM((28, C0, W), BF16),
            pltpu.VMEM((30, 3 * C0, W), BF16),
            pltpu.VMEM((28, 3 * (C1 + C2), W), BF16),
            pltpu.VMEM((11, 3 * C2, W), BF16),
            pltpu.VMEM((18, 3 * C1, W), BF16),
            pltpu.VMEM((C0 * HALF, W), F32),
            pltpu.VMEM((C0, HALF, W), BF16),
            dma, dma, dma, dma, dma((3,)), dma((3,)), dma((3,)), dma((3,)), dma, dma,
        ],
        compiler_params=pltpu.CompilerParams(
            collective_id=0, has_side_effects=True, vmem_limit_bytes=56 << 20
        ),
    )(*args)


def solution(mesh):
    placed = (
        P("region", "chan"),
        P("region", None),
        P("region", None),
        P(None, "chan", None),
        P(None, "chan", None),
        P(None, "chan", None),
        P(),
        P(),
    )
    return jax.shard_map(
        shards, mesh=mesh, in_specs=placed, out_specs=P("chan", "region", None), check_vma=False
    )
```

```python
import jax
import jax.numpy as jnp
from jax import lax
from jax.experimental import pallas as pl
from jax.experimental.pallas import tpu as pltpu
from jax.sharding import PartitionSpec as P

C0 = 64
C1 = 128
C2 = 256
W = 128
HALF = 16
F32 = jnp.float32
BF16 = jnp.bfloat16
MESH = pl.DeviceIdType.MESH

PARTS = (((0, 1, 2), (6, 5)), ((1, 2, 0), (6, 5)), ((2, 0, 1), (5, 5)))
STEPS = (2, 1, 3)


def jobs():
    chunks, start = [[], []], 0
    for p, (_, sizes) in enumerate(PARTS):
        for h, size in enumerate(sizes):
            chunks[h].append((p, W * start, W * (start + size)))
            start += size
    return chunks


def iota(shape, axis):
    return lax.broadcasted_iota(jnp.int32, shape, axis)


def shift(x, step):
    lane = iota(x.shape, 1)
    keep = lane < W - step if step > 0 else lane >= -step
    return jnp.where(keep, pltpu.roll(x, (-step) % W, 1), 0.0)


def silu(v):
    h = 0.5 * v
    return h + h * jnp.tanh(h)


def swap_granules(x):
    rows = x.shape[0]
    row, gran = iota(x.shape, 0), iota(x.shape, 1) // 16
    for s in (1, 2, 4):
        down = pltpu.roll(pltpu.roll(x, 16 * s, 1), rows - s, 0)
        up = pltpu.roll(pltpu.roll(x, W - 16 * s, 1), s, 0)
        row_bit, gran_bit = (row & s) != 0, (gran & s) != 0
        x = jnp.where(row_bit == gran_bit, x, jnp.where(gran_bit, down, up))
    return x


def kernel(
    patches_ref, region_ref, cell_ref, wf_ref, wd_ref, wp_ref, wm_ref, wo_ref,
    out_ref,
    gathered, slots_out, slots_in, sums_out, sums_in, sums_own, tables_out, tables_in, codes_out, codes_in,
    wf_raw, wd_raw, wp_raw, wm_raw, wo_raw,
    wf, wd, wp, wm, wo,
    select, place, grid_f, grid_own, grid, im1, im2, imd, im4, out_f, out_b,
    load, t_send, t_recv, c_send, c_recv, route_send, route_recv,
    w_send, w_recv, g_send, g_recv, o_send, o_recv,
):
    r, c = lax.axis_index("region"), lax.axis_index("chan")
    at = (r // 16, (r // 4) % 4, r % 4)
    other = 1 - c

    def along(axis, step):
        z, y, x = ((at[a] + step) % 4 if a == axis else at[a] for a in range(3))
        return (z * 16 + y * 4 + x, c)

    def remote(src, dst, send, recv, device):
        return pltpu.make_async_remote_copy(
            src_ref=src, dst_ref=dst, send_sem=send, recv_sem=recv,
            device_id=device, device_id_type=MESH,
        )

    def greet(device):
        pl.semaphore_signal(barrier, inc=1, device_id=device, device_id_type=MESH)

    barrier = pltpu.get_barrier_semaphore()
    for axis in range(3):
        for step in STEPS:
            greet(along(axis, step))
    greet((r, other))
    for core in range(2):
        greet(((r + 63 + 2 * c) % 64, core))

    loads = [
        pltpu.make_async_copy(src, dst, load.at[n])
        for n, (src, dst) in enumerate(
            [
                (patches_ref, gathered.at[0]), (wf_ref, wf_raw), (wd_ref, wd_raw),
                (wp_ref, wp_raw), (wm_ref, wm_raw), (wo_ref, wo_raw),
            ]
        )
    ]
    for copy in loads:
        copy.start()

    earlier = (iota((64, 64), 0) < iota((64, 64), 1)).astype(F32).astype(BF16)
    before = jnp.zeros((64, 1), F32)
    entry = jnp.zeros((8, 64), F32)
    for t in range(2):
        target = region_ref[t : t + 1, :]
        hit = jnp.where(iota((64, 64), 0) == target, 1.0, 0.0)
        count = jnp.dot(hit.astype(BF16), earlier, preferred_element_type=F32) + before
        before = before + jnp.sum(hit, axis=1, keepdims=True)
        rank = jnp.sum(hit * count, axis=0, keepdims=True)
        entry = jnp.where(iota((8, 64), 0) == t, target.astype(F32) * 4.0 + rank, entry)
        entry = jnp.where(
            iota((8, 64), 0) == t + 2, cell_ref[t : t + 1, :].astype(F32), entry
        )
    twice = (iota((64, W), 1) % 64 == iota((64, W), 0)).astype(F32).astype(BF16)
    tables_out[...] = jnp.dot(entry.astype(BF16), twice, preferred_element_type=F32)

    chunks = jobs()
    loads[0].wait()
    pl.semaphore_wait(barrier, 12)
    for axis in range(3):
        for step in STEPS:
            remote(
                tables_out, tables_in.at[axis, step], t_send, t_recv.at[axis], along(axis, step)
            ).start()
        tables_in[axis, 0] = tables_out[...]

    def spread_out(phase, h, src, dst):
        for step in STEPS:
            for p, a, b in chunks[h]:
                lanes = pl.ds(a, b - a)
                remote(
                    src(step).at[:, lanes], dst.at[step, :, lanes],
                    route_send.at[phase], route_recv.at[phase, h, p],
                    along(PARTS[p][0][phase], step),
                ).start()

    def arrive(phase, h, p, a, b, dst):
        whole = dst.at[pl.ds(1, 3), :, pl.ds(a, b - a)]
        remote(whole, whole, route_send.at[phase], route_recv.at[phase, h, p], (r, other)).wait_recv()

    for h in range(2):
        spread_out(0, h, lambda step: gathered.at[0], gathered)

    for copy in loads[1:]:
        copy.wait()
    first_rows = pl.ds(pl.multiple_of(64 * c, 64), 64)
    second_rows = pl.ds(pl.multiple_of(128 * c, 128), 128)
    wf[first_rows, :] = jnp.concatenate([wf_raw[k] for k in range(9)], axis=1)
    for k in range(9):
        wd[second_rows, 128 * k : 128 * k + 128] = wd_raw[k]
        wp[second_rows, 256 * k : 256 * k + 256] = wp_raw[k]
    weight_copies = [
        remote(buf.at[rows], buf.at[rows], w_send.at[n], w_recv.at[n], (r, other))
        for n, (buf, rows) in enumerate([(wf, first_rows), (wd, second_rows), (wp, second_rows)])
    ]
    for copy in weight_copies:
        copy.start()
    for k in range(9):
        i, j = k // 3, k % 3
        wm[:, 1152 * i + 128 * j : 1152 * i + 128 * j + 128] = wm_raw[k, :, :C1]
        wm[:, 1152 * i + 384 + 256 * j : 1152 * i + 384 + 256 * j + 256] = wm_raw[k, :, C1:]
        wo[:, 128 * k : 128 * k + 128] = wo_raw[k]

    lane = iota((8, W), 1)
    left = lane < 64
    for p, (axes, _) in enumerate(PARTS):
        here, second, third = axes
        three = tables_in.at[here, pl.ds(1, 3)]
        remote(three, three, t_send, t_recv.at[here], (r, other)).wait_recv()
        values = jnp.zeros((8, 256), F32)
        for half in range(2):
            table = jnp.where(left, tables_in[here, 2 * half], tables_in[here, 2 * half + 1])
            code = table.astype(jnp.int32)
            region = code // 4
            place_of = (region // 16, (region // 4) % 4, region % 4)
            slot = (
                ((place_of[second] - at[second]) & 3) * 64
                + (2 * half + lane // 64) * 16
                + ((place_of[third] - at[third]) & 3) * 4
                + code % 4
            )
            slot = jnp.where(place_of[here] == at[here], slot, -1)
            hits = [iota((256, W), 0) == slot[t : t + 1] for t in range(2)]
            select[p, :, W * half : W * half + W] = (
                jnp.where(jnp.logical_or(hits[0], hits[1]), 1.0, 0.0).astype(BF16)
            )
            for t in range(2):
                cells = jnp.broadcast_to(table[t + 2 : t + 3] + 1.0, (8, W)).astype(BF16)
                values = values + lax.dot_general(
                    cells, jnp.where(hits[t], 1.0, 0.0).astype(BF16),
                    (((1,), (1,)), ((), ())), preferred_element_type=F32,
                )
        for step in range(4):
            value = values[:, W * (step // 2) : W * (step // 2) + W]
            turned = pltpu.roll(value, 64, 1)
            value = jnp.where(left, value, turned) if step % 2 == 0 else jnp.where(left, turned, value)
            value = jnp.where(value > 0.0, value - 1.0 + (32 * ((lane // 4) % 4)).astype(F32), -1.0)
            if step == 0:
                codes_in[p, 0] = value
            else:
                codes_out[p, step] = value
        for step in STEPS:
            remote(
                codes_out.at[p, step], codes_in.at[p, step], c_send, c_recv.at[p], along(second, step)
            ).start()

    for h in range(2):
        for p, a, b in chunks[h]:
            arrive(0, h, p, a, b, gathered)
            for n in range(a, b, 256):
                e = min(n + 256, b)
                slots = jnp.dot(
                    select[p], gathered[:, :, n:e].reshape(256, e - n), preferred_element_type=F32
                ).astype(BF16)
                slots_in[0, :, n:e] = slots[:64]
                slots_out[:, :, n:e] = slots[64:].reshape(3, 64, e - n)
        spread_out(1, h, lambda step: slots_out.at[step - 1], slots_in)

    for p in range(3):
        three = codes_in.at[p, pl.ds(1, 3)]
        remote(three, three, c_send, c_recv.at[p], (r, other)).wait_recv()
        for half in range(2):
            code = jnp.where(left, codes_in[p, 2 * half], codes_in[p, 2 * half + 1])[0:1]
            place[p, :, W * half : W * half + W] = jnp.where(
                iota((W, W), 0).astype(F32) == code, 1.0, 0.0
            ).astype(BF16)
    for h in range(2):
        for p, a, b in chunks[h]:
            arrive(1, h, p, a, b, slots_in)
            for n in range(a, b, 256):
                e = min(n + 256, b)
                sums = jnp.dot(
                    place[p], slots_in[:, :, n:e].reshape(256, e - n), preferred_element_type=F32
                )
                sums_own[:, n:e] = sums[:32]
                sums_out[:, :, n:e] = sums[32:].astype(BF16).reshape(3, 32, e - n)
        spread_out(2, h, lambda step: sums_out.at[step - 1], sums_in)

    for h in range(2):
        for p, a, b in chunks[h]:
            arrive(2, h, p, a, b, sums_in)
            total = sums_own[:, a:b]
            for step in STEPS:
                total = total + sums_in[step, :, a:b].astype(F32)
            for n in range(a, b, W):
                block = swap_granules(total[:, n - a : n - a + W])
                for band in range(4):
                    grid_f[pl.ds(256 * band + n // W, 8, stride=32), :] = block[8 * band : 8 * band + 8]
    grid_own[...] = grid_f[...].astype(BF16).reshape(32, 32, W)

    own = pl.ds(pl.multiple_of(32 * c, 32), 32)
    grid_copies = [
        remote(
            grid_own.at[pl.ds(10 * other, 22)], grid.at[pl.ds(6 * c, 22), own],
            g_send.at[0], g_recv.at[2], (r, other),
        ),
        remote(
            grid_own.at[pl.ds(26, 6)], grid.at[pl.ds(0, 6), own],
            g_send.at[1], g_recv.at[c], ((r + 1) % 64, 0),
        ),
        remote(
            grid_own.at[pl.ds(0, 6)], grid.at[pl.ds(22, 6), own],
            g_send.at[2], g_recv.at[c], ((r + 63) % 64, 1),
        ),
    ]
    for copy in grid_copies:
        copy.start()
    grid[pl.ds(6 * other, 22), own, :] = grid_own[pl.ds(10 * c, 22)]
    grid_copies[0].wait_recv()
    top = jnp.logical_and(r == 0, c == 0)
    bottom = jnp.logical_and(r == 63, c == 1)
    keep_top = jnp.where(top, 0.0, 1.0)
    keep_bottom = jnp.where(bottom, 0.0, 1.0)
    even = iota((C2, W), 1) % 2 == 0

    def cols(x):
        return jnp.concatenate([shift(x, -1), x, shift(x, 1)], axis=0)

    def widen(l):
        im1[l] = cols(grid[l].astype(F32)).astype(BF16)

    def first_rows_of(k, _):
        f = 4 * ((k + 2 * other) % 7)
        window = jnp.concatenate(
            [im1[pl.ds(f + t, 3)].reshape(576, W) for t in range(4)], axis=1
        )
        total = jnp.dot(wf[...], window, preferred_element_type=F32)
        for t in range(4):
            factor = jnp.where(f + t < 5, keep_top, jnp.where(f + t >= 21, keep_bottom, 1.0))
            row = silu(total[:, W * t : W * t + W]) * factor
            im2[f + t, 0:384] = cols(row).astype(BF16)
        return 0

    def widen_own(l, _):
        widen(6 * other + l)
        return 0

    lax.fori_loop(0, 22, widen_own, 0, unroll=2)
    for copy in weight_copies:
        copy.wait_recv()
    lax.fori_loop(0, 5, first_rows_of, 0)
    for n in range(2):
        remote(
            grid_own.at[pl.ds(0, 6)], grid.at[pl.ds(0, 6), pl.ds(0, 32)],
            g_send.at[1], g_recv.at[n], (r, other),
        ).wait_recv()

    @pl.when(top)
    def _():
        grid[0:6] = jnp.zeros((6, C0, W), BF16)

    @pl.when(bottom)
    def _():
        grid[22:28] = jnp.zeros((6, C0, W), BF16)

    for l in range(6):
        widen(22 * c + l)
    lax.fori_loop(5, 7, first_rows_of, 0)

    def spread_pair(x):
        return jnp.concatenate([shift(x, -2), x, shift(x, 2)], axis=0).astype(BF16)

    pairs = []
    for m in range(6):
        window = jnp.concatenate(
            [
                jnp.concatenate([im2[4 * m + 2 * t + i, 0:384] for i in range(3)], axis=0)
                for t in range(2)
            ],
            axis=1,
        )
        total = jnp.dot(wd[...], window, preferred_element_type=F32)
        pair = silu(jnp.where(even, total[:, :W], pltpu.roll(total[:, W:], 1, 1)))
        if m == 0:
            pair = pair * keep_top
        if m == 5:
            pair = pair * keep_bottom
        pair = pair.astype(BF16).astype(F32)
        imd[2 * m] = spread_pair(pair)
    for m in range(5):
        a = imd[2 * m, C2 : 2 * C2].astype(F32)
        b = imd[2 * m + 2, C2 : 2 * C2].astype(F32)
        imd[2 * m + 1] = spread_pair(jnp.where(even, shift(a, 1), shift(b, -1)))

    for ms in ((0, 1), (2, 3), (4,)):
        window = jnp.concatenate([imd[2 * m : 2 * m + 3].reshape(2304, W) for m in ms], axis=1)
        total = jnp.dot(wp[...], window, preferred_element_type=F32)
        for t, m in enumerate(ms):
            third = silu(total[:, W * t : W * t + W]) + imd[2 * m + 1, C2 : 2 * C2].astype(F32)
            if m == 0:
                third = jnp.where(even, third * keep_top, third)
            if m == 4:
                third = jnp.where(even, third, third * keep_bottom)
            l1, l2, r1, r2 = shift(third, -1), shift(third, -2), shift(third, 1), shift(third, 2)
            edge = iota((C2, W), 1) < W - 1
            ups = (
                (
                    jnp.where(even, l2, l1),
                    jnp.where(even, third, l1),
                    jnp.where(edge, jnp.where(even, third, r1), 0.0),
                ),
                (
                    jnp.where(even, l1, third),
                    jnp.where(even, r1, third),
                    jnp.where(even, r1, r2),
                ),
            )
            for half in range(2):
                for j in range(3):
                    value = ups[half][j].astype(BF16)
                    if half == 0 and j == 0:
                        value = jnp.where(iota((C2, W), 1) == 0, 0.0, ups[half][j]).astype(BF16)
                    f = 4 * m + 3 + 2 * half
                    im2[f, 384 + C2 * j : 384 + C2 * j + C2] = value
                    im2[f + 1, 384 + C2 * j : 384 + C2 * j + C2] = value

    def fourth_rows(n, _):
        g = 2 * n
        window = jnp.concatenate(
            [im2[pl.ds(g + 3 + t, 3)].reshape(3456, W) for t in range(2)], axis=1
        )
        total = jnp.dot(wm[...], window, preferred_element_type=F32)
        for t in range(2):
            factor = jnp.where(g + t < 1, keep_top, jnp.where(g + t >= 17, keep_bottom, 1.0))
            im4[g + t] = cols(silu(total[:, W * t : W * t + W]) * factor).astype(BF16)
        return 0

    lax.fori_loop(0, 9, fourth_rows, 0)

    def out_rows(n, _):
        f = 4 * n
        window = jnp.concatenate(
            [im4[pl.ds(f + t, 3)].reshape(1152, W) for t in range(4)], axis=1
        )
        total = jnp.dot(wo[...], window, preferred_element_type=F32)
        for t in range(4):
            row = total[:, W * t : W * t + W] + grid[f + t + 6].astype(F32)
            out_f[pl.ds(f + t, C0, stride=HALF), :] = row
        return 0

    lax.fori_loop(0, 4, out_rows, 0)
    out_b[...] = out_f[...].astype(BF16).reshape(C0, HALF, W)
    mine = pl.ds(pl.multiple_of(HALF * c, HALF), HALF)
    out_copy = remote(
        out_b.at[pl.ds(32 * other, 32)], out_ref.at[:, mine, :], o_send, o_recv, (r, other)
    )
    out_copy.start()
    out_ref[:, mine, :] = out_b[pl.ds(32 * c, 32)]

    for copy in weight_copies + grid_copies:
        copy.wait_send()
    for phase, buffer in enumerate((gathered, slots_in, sums_in)):
        whole = buffer.at[pl.ds(1, 3)]
        remote(whole, whole, route_send.at[phase], o_recv, (r, other)).wait_send()
    three = tables_in.at[:, pl.ds(1, 3)]
    remote(three, three, t_send, o_recv, (r, other)).wait_send()
    three = codes_in.at[:, pl.ds(1, 3)]
    remote(three, three, c_send, o_recv, (r, other)).wait_send()
    out_copy.wait()


def shards(patches, region, cell, *weights):
    vmem = pl.BlockSpec(memory_space=pltpu.VMEM)
    anywhere = pl.BlockSpec(memory_space=pl.ANY)
    dma = pltpu.SemaphoreType.DMA
    return pl.pallas_call(
        kernel,
        out_shape=jax.ShapeDtypeStruct((32, 32, W), BF16),
        in_specs=[anywhere, vmem, vmem] + [anywhere] * 5,
        out_specs=vmem,
        scratch_shapes=[
            pltpu.VMEM((4, 64, 4096), BF16),
            pltpu.VMEM((3, 64, 4096), BF16),
            pltpu.VMEM((4, 64, 4096), BF16),
            pltpu.VMEM((3, 32, 4096), BF16),
            pltpu.VMEM((4, 32, 4096), BF16),
            pltpu.VMEM((32, 4096), F32),
            pltpu.VMEM((8, W), F32),
            pltpu.VMEM((3, 4, 8, W), F32),
            pltpu.VMEM((3, 4, 8, W), F32),
            pltpu.VMEM((3, 4, 8, W), F32),
            pltpu.VMEM((9, 64, C0), BF16),
            pltpu.VMEM((9, 128, C1), BF16),
            pltpu.VMEM((9, 128, C2), BF16),
            pltpu.VMEM((9, C1, C1 + C2), BF16),
            pltpu.VMEM((9, C0, C1), BF16),
            pltpu.VMEM((C1, 9 * C0), BF16),
            pltpu.VMEM((C2, 9 * C1), BF16),
            pltpu.VMEM((C2, 9 * C2), BF16),
            pltpu.VMEM((C1, 9 * (C1 + C2)), BF16),
            pltpu.VMEM((C0, 9 * C1), BF16),
            pltpu.VMEM((3, 256, 256), BF16),
            pltpu.VMEM((3, W, 256), BF16),
            pltpu.VMEM((1024, W), F32),
            pltpu.VMEM((32, 32, W), BF16),
            pltpu.VMEM((28, C0, W), BF16),
            pltpu.VMEM((30, 3 * C0, W), BF16),
            pltpu.VMEM((28, 3 * (C1 + C2), W), BF16),
            pltpu.VMEM((11, 3 * C2, W), BF16),
            pltpu.VMEM((18, 3 * C1, W), BF16),
            pltpu.VMEM((C0 * HALF, W), F32),
            pltpu.VMEM((C0, HALF, W), BF16),
            dma((6,)), dma, dma((3,)), dma, dma((3,)), dma((3,)), dma((3, 2, 3)),
            dma((3,)), dma((3,)), dma((3,)), dma((3,)), dma, dma,
        ],
        compiler_params=pltpu.CompilerParams(
            collective_id=0, has_side_effects=True, vmem_limit_bytes=56 << 20
        ),
    )(patches, region.T, cell.T, *weights)


def solution(mesh):
    placed = (
        P("region", "chan"),
        P("region", None),
        P("region", None),
        P(None, "chan", None),
        P(None, "chan", None),
        P(None, "chan", None),
        P(),
        P(),
    )
    return jax.shard_map(
        shards, mesh=mesh, in_specs=placed, out_specs=P("chan", "region", None), check_vma=False
    )
```

```python
import jax
import jax.numpy as jnp
from jax import lax
from jax.experimental import pallas as pl
from jax.experimental.pallas import tpu as pltpu
from jax.sharding import PartitionSpec as P

C0 = 64
C1 = 128
C2 = 256
W = 128
HALF = 16
F32 = jnp.float32
BF16 = jnp.bfloat16
MESH = pl.DeviceIdType.MESH

PARTS = (((0, 1, 2), (6, 3, 2)), ((1, 2, 0), (5, 3, 3)), ((2, 0, 1), (5, 2, 3)))
STEPS = (2, 1, 3)


def jobs():
    chunks, start = [], 0
    for h in range(3):
        chunks.append([])
        for p, (_, sizes) in enumerate(PARTS):
            chunks[h].append((p, W * start, W * (start + sizes[h])))
            start += sizes[h]
    return chunks


def iota(shape, axis):
    return lax.broadcasted_iota(jnp.int32, shape, axis)


def shift(x, step):
    lane = iota(x.shape, 1)
    keep = lane < W - step if step > 0 else lane >= -step
    return jnp.where(keep, pltpu.roll(x, (-step) % W, 1), jnp.zeros_like(x))


def silu(v):
    h = 0.5 * v
    return h + h * jnp.tanh(h)


def swap_granules(x):
    rows = x.shape[0]
    row, gran = iota(x.shape, 0), iota(x.shape, 1) // 16
    for s in (1, 2, 4):
        down = pltpu.roll(pltpu.roll(x, 16 * s, 1), rows - s, 0)
        up = pltpu.roll(pltpu.roll(x, W - 16 * s, 1), s, 0)
        row_bit, gran_bit = (row & s) != 0, (gran & s) != 0
        x = jnp.where(row_bit == gran_bit, x, jnp.where(gran_bit, down, up))
    return x


def kernel(
    patches_ref, region_ref, cell_ref, wf_ref, wd_ref, wp_ref, wm_ref, wo_ref,
    out_ref,
    gathered, slots_out, slots_in, sums_out, sums_in, sums_own, tables_out, tables_in, codes_out, codes_in,
    wf_raw, wd_raw, wp_raw, wm_raw, wo_raw,
    wf, wd, wp, wm, wo,
    select, place, grid_f, tile, halo, im1, im2, imd, im4, out_f, out_b,
    load, t_send, t_recv, c_send, c_recv, route_send, route_recv,
    w_send, w_recv, x_send, x_recv, h_send, h_recv, o_send, o_recv,
):
    r, c = lax.axis_index("region"), lax.axis_index("chan")
    at = (r // 16, (r // 4) % 4, r % 4)
    other = 1 - c

    def along(axis, step):
        z, y, x = ((at[a] + step) % 4 if a == axis else at[a] for a in range(3))
        return (z * 16 + y * 4 + x, c)

    def remote(src, dst, send, recv, device):
        return pltpu.make_async_remote_copy(
            src_ref=src, dst_ref=dst, send_sem=send, recv_sem=recv,
            device_id=device, device_id_type=MESH,
        )

    def greet(device):
        pl.semaphore_signal(barrier, inc=1, device_id=device, device_id_type=MESH)

    barrier = pltpu.get_barrier_semaphore()
    for axis in range(3):
        for step in STEPS:
            greet(along(axis, step))
    greet((r, other))

    loads = [
        pltpu.make_async_copy(src, dst, load.at[n])
        for n, (src, dst) in enumerate(
            [
                (patches_ref, gathered.at[0]), (wf_ref, wf_raw), (wd_ref, wd_raw),
                (wp_ref, wp_raw), (wm_ref, wm_raw), (wo_ref, wo_raw),
            ]
        )
    ]
    for copy in loads:
        copy.start()

    earlier = (iota((64, 64), 0) < iota((64, 64), 1)).astype(F32).astype(BF16)
    before = jnp.zeros((64, 1), F32)
    entry = jnp.zeros((8, 64), F32)
    for t in range(2):
        target = region_ref[t : t + 1, :]
        hit = jnp.where(iota((64, 64), 0) == target, 1.0, 0.0)
        count = jnp.dot(hit.astype(BF16), earlier, preferred_element_type=F32) + before
        before = before + jnp.sum(hit, axis=1, keepdims=True)
        rank = jnp.sum(hit * count, axis=0, keepdims=True)
        entry = jnp.where(iota((8, 64), 0) == t, target.astype(F32) * 4.0 + rank, entry)
        entry = jnp.where(
            iota((8, 64), 0) == t + 2, cell_ref[t : t + 1, :].astype(F32), entry
        )
    twice = (iota((64, W), 1) % 64 == iota((64, W), 0)).astype(F32).astype(BF16)
    tables_out[...] = jnp.dot(entry.astype(BF16), twice, preferred_element_type=F32)

    chunks = jobs()
    loads[0].wait()
    pl.semaphore_wait(barrier, 10)
    for axis in range(3):
        for step in STEPS:
            remote(
                tables_out, tables_in.at[axis, step], t_send, t_recv.at[axis], along(axis, step)
            ).start()
        tables_in[axis, 0] = tables_out[...]

    def spread_out(phase, h, src, dst):
        for step in STEPS:
            for p, a, b in chunks[h]:
                lanes = pl.ds(a, b - a)
                remote(
                    src(step).at[:, lanes], dst.at[step, :, lanes],
                    route_send.at[phase], route_recv.at[phase, h, p],
                    along(PARTS[p][0][phase], step),
                ).start()

    def arrive(phase, h, p, a, b, dst):
        whole = dst.at[pl.ds(1, 3), :, pl.ds(a, b - a)]
        remote(whole, whole, route_send.at[phase], route_recv.at[phase, h, p], (r, other)).wait_recv()

    for h in range(3):
        spread_out(0, h, lambda step: gathered.at[0], gathered)

    for copy in loads[1:]:
        copy.wait()
    first_rows = pl.ds(pl.multiple_of(64 * c, 64), 64)
    second_rows = pl.ds(pl.multiple_of(128 * c, 128), 128)
    wf[first_rows, :] = jnp.concatenate([wf_raw[k] for k in range(9)], axis=1)
    for k in range(9):
        wd[second_rows, 128 * k : 128 * k + 128] = wd_raw[k]
        wp[second_rows, 256 * k : 256 * k + 256] = wp_raw[k]
    weight_copies = [
        remote(buf.at[rows], buf.at[rows], w_send.at[n], w_recv.at[n], (r, other))
        for n, (buf, rows) in enumerate([(wf, first_rows), (wd, second_rows), (wp, second_rows)])
    ]
    for copy in weight_copies:
        copy.start()
    for k in range(9):
        i, j = k // 3, k % 3
        wm[:, 1152 * i + 128 * j : 1152 * i + 128 * j + 128] = wm_raw[k, :, :C1]
        wm[:, 1152 * i + 384 + 256 * j : 1152 * i + 384 + 256 * j + 256] = wm_raw[k, :, C1:]
        wo[:, 128 * k : 128 * k + 128] = wo_raw[k]

    lane = iota((8, W), 1)
    left = lane < 64
    for p, (axes, _) in enumerate(PARTS):
        here, second, third = axes
        three = tables_in.at[here, pl.ds(1, 3)]
        remote(three, three, t_send, t_recv.at[here], (r, other)).wait_recv()
        values = jnp.zeros((8, 256), F32)
        for half in range(2):
            table = jnp.where(left, tables_in[here, 2 * half], tables_in[here, 2 * half + 1])
            code = table.astype(jnp.int32)
            region = code // 4
            place_of = (region // 16, (region // 4) % 4, region % 4)
            slot = (
                ((place_of[second] - at[second]) & 3) * 64
                + (2 * half + lane // 64) * 16
                + ((place_of[third] - at[third]) & 3) * 4
                + code % 4
            )
            slot = jnp.where(place_of[here] == at[here], slot, -1)
            hits = [iota((256, W), 0) == slot[t : t + 1] for t in range(2)]
            select[p, :, W * half : W * half + W] = (
                jnp.where(jnp.logical_or(hits[0], hits[1]), 1.0, 0.0).astype(BF16)
            )
            for t in range(2):
                cells = jnp.broadcast_to(table[t + 2 : t + 3] + 1.0, (8, W)).astype(BF16)
                values = values + lax.dot_general(
                    cells, jnp.where(hits[t], 1.0, 0.0).astype(BF16),
                    (((1,), (1,)), ((), ())), preferred_element_type=F32,
                )
        for step in range(4):
            value = values[:, W * (step // 2) : W * (step // 2) + W]
            turned = pltpu.roll(value, 64, 1)
            value = jnp.where(left, value, turned) if step % 2 == 0 else jnp.where(left, turned, value)
            value = jnp.where(value > 0.0, value - 1.0 + (32 * ((lane // 4) % 4)).astype(F32), -1.0)
            if step == 0:
                codes_in[p, 0] = value
            else:
                codes_out[p, step] = value
        for step in STEPS:
            remote(
                codes_out.at[p, step], codes_in.at[p, step], c_send, c_recv.at[p], along(second, step)
            ).start()

    for h in range(3):
        for p, a, b in chunks[h]:
            arrive(0, h, p, a, b, gathered)
            for n in range(a, b, 256):
                e = min(n + 256, b)
                slots = jnp.dot(
                    select[p], gathered[:, :, n:e].reshape(256, e - n), preferred_element_type=F32
                ).astype(BF16)
                slots_in[0, :, n:e] = slots[:64]
                slots_out[:, :, n:e] = slots[64:].reshape(3, 64, e - n)
        spread_out(1, h, lambda step: slots_out.at[step - 1], slots_in)

    for p in range(3):
        three = codes_in.at[p, pl.ds(1, 3)]
        remote(three, three, c_send, c_recv.at[p], (r, other)).wait_recv()
        for half in range(2):
            code = jnp.where(left, codes_in[p, 2 * half], codes_in[p, 2 * half + 1])[0:1]
            place[p, :, W * half : W * half + W] = jnp.where(
                iota((W, W), 0).astype(F32) == code, 1.0, 0.0
            ).astype(BF16)
    for h in range(3):
        for p, a, b in chunks[h]:
            arrive(1, h, p, a, b, slots_in)
            for n in range(a, b, 256):
                e = min(n + 256, b)
                sums = jnp.dot(
                    place[p], slots_in[:, :, n:e].reshape(256, e - n), preferred_element_type=F32
                )
                sums_own[:, n:e] = sums[:32]
                sums_out[:, :, n:e] = sums[32:].astype(BF16).reshape(3, 32, e - n)
        spread_out(2, h, lambda step: sums_out.at[step - 1], sums_in)

    top = jnp.logical_and(r == 0, c == 0)
    bottom = jnp.logical_and(r == 63, c == 1)
    keep_top = jnp.where(top, 0.0, 1.0)
    keep_bottom = jnp.where(bottom, 0.0, 1.0)
    even = iota((C2, W), 1) % 2 == 0

    def taps(x):
        return shift(x, -1), x, shift(x, 1)

    def settle(e):
        mine = pl.ds(pl.multiple_of(32 * c + 16 * e, 16), 16)
        tile[:, mine, :] = grid_f[e].astype(BF16).reshape(32, 16, W)
        copy = remote(tile.at[:, mine], tile.at[:, mine], x_send.at[e], x_recv.at[e], (r, other))
        copy.start()
        return copy

    own_rows = tile.at[pl.ds(10 * c, 22)]
    own_im1 = im1.at[pl.ds(6 * other, 22)]

    def widen(e, core):
        source = own_rows.at[:, pl.ds(pl.multiple_of(32 * core + 16 * e, 16), 16)]
        target = [
            own_im1.at[:, pl.ds(pl.multiple_of(C0 * j + 32 * core + 16 * e, 16), 16)]
            for j in range(3)
        ]
        for l in range(22):
            for j, tap in enumerate(taps(source[l])):
                target[j][l] = tap

    tile_copies = []
    for h in range(3):
        for p, a, b in chunks[h]:
            arrive(2, h, p, a, b, sums_in)
            total = sums_own[:, a:b]
            for step in STEPS:
                total = total + sums_in[step, :, a:b].astype(F32)
            for n in range(a, b, W):
                block = swap_granules(total[:, n - a : n - a + W])
                e, ch = n // W // 16, n // W % 16
                for band in range(4):
                    grid_f[e, pl.ds(W * band + ch, 8, stride=16), :] = block[8 * band : 8 * band + 8]
        if h != 1:
            e = h // 2
            tile_copies.append(settle(e))
            widen(e, c)
            tile_copies[e].wait_recv()
            if e == 1:
                halo_copy = remote(
                    tile.at[pl.ds(26 * other, 6)], halo, h_send, h_recv, ((r + 1 + 62 * c) % 64, c)
                )
                halo_copy.start()
            widen(e, other)
    for copy in weight_copies:
        copy.wait_recv()

    def first_rows_of(base, n, source, target):
        f = 4 * n
        window = jnp.concatenate(
            [source[f + t : f + t + 3].reshape(576, W) for t in range(4)], axis=1
        )
        total = jnp.dot(wf[...], window, preferred_element_type=F32)
        for t in range(4):
            at_row = base + f + t
            factor = jnp.where(at_row < 5, keep_top, jnp.where(at_row >= 21, keep_bottom, 1.0))
            row = (silu(total[:, W * t : W * t + W]) * factor).astype(BF16)
            for j, tap in enumerate(taps(row)):
                target[f + t, C1 * j : C1 * j + C1] = tap

    def spread_pair(target, at_pair, x):
        for j, tap in enumerate((shift(x, -2), x, shift(x, 2))):
            target[at_pair, C2 * j : C2 * j + C2] = tap

    def second_pair(base, m, source, target):
        window = jnp.concatenate(
            [
                jnp.concatenate([source[4 * m + 2 * t + i, 0:384] for i in range(3)], axis=0)
                for t in range(2)
            ],
            axis=1,
        )
        total = jnp.dot(wd[...], window, preferred_element_type=F32)
        pair = silu(jnp.where(even, total[:, :W], pltpu.roll(total[:, W:], 1, 1)))
        at_pair = base + m
        factor = jnp.where(at_pair == 0, keep_top, jnp.where(at_pair == 5, keep_bottom, 1.0))
        spread_pair(target, 2 * m, (pair * factor).astype(BF16))

    def blend(m, target):
        a, b = target[2 * m, C2 : 2 * C2], target[2 * m + 2, C2 : 2 * C2]
        spread_pair(target, 2 * m + 1, jnp.where(even, shift(a, 1), shift(b, -1)))

    def third_pairs(base, ms, source, target):
        window = jnp.concatenate(
            [source[2 * m : 2 * m + 3].reshape(2304, W) for m in ms], axis=1
        )
        total = jnp.dot(wp[...], window, preferred_element_type=F32)
        for t, m in enumerate(ms):
            third = silu(total[:, W * t : W * t + W]) + source[2 * m + 1, C2 : 2 * C2].astype(F32)
            factor = jnp.where(
                even,
                jnp.where(base + m == 0, keep_top, 1.0),
                jnp.where(base + m == 4, keep_bottom, 1.0),
            )
            third = (third * factor).astype(BF16)
            l1, l2, r1, r2 = shift(third, -1), shift(third, -2), shift(third, 1), shift(third, 2)
            lane = iota((C2, W), 1)
            ups = (
                (
                    jnp.where(even, l2, l1),
                    jnp.where(even, third, l1),
                    jnp.where(lane == W - 1, jnp.zeros_like(third), jnp.where(even, third, r1)),
                ),
                (
                    jnp.where(lane == 0, jnp.zeros_like(third), jnp.where(even, l1, third)),
                    jnp.where(even, r1, third),
                    jnp.where(even, r1, r2),
                ),
            )
            for half in range(2):
                for j in range(3):
                    f = 4 * m + 3 + 2 * half
                    target[f, 384 + C2 * j : 384 + C2 * j + C2] = ups[half][j]
                    target[f + 1, 384 + C2 * j : 384 + C2 * j + C2] = ups[half][j]

    def fourth_rows(base, n, source, target):
        g = 2 * n
        window = jnp.concatenate(
            [source[g + 3 + t : g + 6 + t].reshape(3456, W) for t in range(2)], axis=1
        )
        total = jnp.dot(wm[...], window, preferred_element_type=F32)
        for t in range(2):
            at_row = base + g + t
            factor = jnp.where(at_row < 1, keep_top, jnp.where(at_row >= 17, keep_bottom, 1.0))
            row = (silu(total[:, W * t : W * t + W]) * factor).astype(BF16)
            for j, tap in enumerate(taps(row)):
                target[g + t, C1 * j : C1 * j + C1] = tap

    def out_rows(n, source, skip, target):
        f = 4 * n
        window = jnp.concatenate(
            [source[f + t : f + t + 3].reshape(1152, W) for t in range(4)], axis=1
        )
        total = jnp.dot(wo[...], window, preferred_element_type=F32)
        for t in range(4):
            row = total[:, W * t : W * t + W] + skip[f + t].astype(F32)
            target[pl.ds(f + t, C0, stride=8), :] = row

    base = 8 * other
    at_first, at_im2 = im1.at[pl.ds(base, 22)], im2.at[pl.ds(base, 20)]
    at_imd, at_im4 = imd.at[pl.ds(4 * other, 7)], im4.at[pl.ds(base, 10)]
    for n in range(5):
        first_rows_of(base, n, at_first, at_im2)
    for m in range(4):
        second_pair(2 * other, m, at_im2, at_imd)
    for m in range(3):
        blend(m, at_imd)
    third_pairs(2 * other, [0, 1], at_imd, at_im2)
    third_pairs(2 * other, [2], at_imd, at_im2)
    for n in range(5):
        fourth_rows(base, n, at_im2, at_im4)
    for n in range(2):
        out_rows(n, at_im4, tile.at[pl.ds(8 + 8 * c, 8)], out_f.at[other])
    halo_copy.wait_recv()

    @pl.when(jnp.logical_or(top, bottom))
    def _():
        halo[...] = jnp.zeros((6, C0, W), BF16)

    at_first, at_im2 = im1.at[pl.ds(22 * c, 6)], im2.at[pl.ds(20 * c, 8)]
    for l in range(6):
        for j, tap in enumerate(taps(halo[l])):
            at_first[l, C0 * j : C0 * j + C0] = tap
    at_first = im1.at[pl.ds(20 * c, 10)]
    for n in range(2):
        first_rows_of(20 * c, n, at_first, at_im2)
    at_im2, at_imd = im2.at[pl.ds(16 * c, 9)], imd.at[pl.ds(8 * c, 3)]
    for m in range(2):
        second_pair(4 * c, m, at_im2, at_imd)
    at_im2, at_imd = im2.at[pl.ds(12 * c, 11)], imd.at[pl.ds(6 * c, 5)]
    for m in range(2):
        blend(m, at_imd)
    third_pairs(3 * c, [0, 1], at_imd, at_im2)
    at_im2, at_im4 = im2.at[pl.ds(10 * c, 13)], im4.at[pl.ds(10 * c, 8)]
    for n in range(4):
        fourth_rows(10 * c, n, at_im2, at_im4)
    at_im4 = im4.at[pl.ds(8 * c, 10)]
    for n in range(2):
        out_rows(n, at_im4, tile.at[pl.ds(24 * c, 8)], out_f.at[c])
    out_b[...] = jnp.concatenate(
        [out_f[n].reshape(C0, 8, W) for n in range(2)], axis=1
    ).astype(BF16)
    mine = pl.ds(pl.multiple_of(HALF * c, HALF), HALF)
    out_copy = remote(
        out_b.at[pl.ds(32 * other, 32)], out_ref.at[:, mine, :], o_send, o_recv, (r, other)
    )
    out_copy.start()
    out_ref[:, mine, :] = out_b[pl.ds(32 * c, 32)]

    for copy in weight_copies + tile_copies + [halo_copy]:
        copy.wait_send()
    for phase, buffer in enumerate((gathered, slots_in, sums_in)):
        whole = buffer.at[pl.ds(1, 3)]
        remote(whole, whole, route_send.at[phase], o_recv, (r, other)).wait_send()
    three = tables_in.at[:, pl.ds(1, 3)]
    remote(three, three, t_send, o_recv, (r, other)).wait_send()
    three = codes_in.at[:, pl.ds(1, 3)]
    remote(three, three, c_send, o_recv, (r, other)).wait_send()
    out_copy.wait()


def shards(patches, region, cell, *weights):
    vmem = pl.BlockSpec(memory_space=pltpu.VMEM)
    anywhere = pl.BlockSpec(memory_space=pl.ANY)
    dma = pltpu.SemaphoreType.DMA
    return pl.pallas_call(
        kernel,
        out_shape=jax.ShapeDtypeStruct((32, 32, W), BF16),
        in_specs=[anywhere, vmem, vmem] + [anywhere] * 5,
        out_specs=vmem,
        scratch_shapes=[
            pltpu.VMEM((4, 64, 4096), BF16),
            pltpu.VMEM((3, 64, 4096), BF16),
            pltpu.VMEM((4, 64, 4096), BF16),
            pltpu.VMEM((3, 32, 4096), BF16),
            pltpu.VMEM((4, 32, 4096), BF16),
            pltpu.VMEM((32, 4096), F32),
            pltpu.VMEM((8, W), F32),
            pltpu.VMEM((3, 4, 8, W), F32),
            pltpu.VMEM((3, 4, 8, W), F32),
            pltpu.VMEM((3, 4, 8, W), F32),
            pltpu.VMEM((9, 64, C0), BF16),
            pltpu.VMEM((9, 128, C1), BF16),
            pltpu.VMEM((9, 128, C2), BF16),
            pltpu.VMEM((9, C1, C1 + C2), BF16),
            pltpu.VMEM((9, C0, C1), BF16),
            pltpu.VMEM((C1, 9 * C0), BF16),
            pltpu.VMEM((C2, 9 * C1), BF16),
            pltpu.VMEM((C2, 9 * C2), BF16),
            pltpu.VMEM((C1, 9 * (C1 + C2)), BF16),
            pltpu.VMEM((C0, 9 * C1), BF16),
            pltpu.VMEM((3, 256, 256), BF16),
            pltpu.VMEM((3, W, 256), BF16),
            pltpu.VMEM((2, 512, W), F32),
            pltpu.VMEM((32, C0, W), BF16),
            pltpu.VMEM((6, C0, W), BF16),
            pltpu.VMEM((30, 3 * C0, W), BF16),
            pltpu.VMEM((28, 3 * (C1 + C2), W), BF16),
            pltpu.VMEM((11, 3 * C2, W), BF16),
            pltpu.VMEM((18, 3 * C1, W), BF16),
            pltpu.VMEM((2, C0 * 8, W), F32),
            pltpu.VMEM((C0, HALF, W), BF16),
            dma((6,)), dma, dma((3,)), dma, dma((3,)), dma((3,)), dma((3, 3, 3)),
            dma((3,)), dma((3,)), dma((2,)), dma((2,)), dma, dma, dma, dma,
        ],
        compiler_params=pltpu.CompilerParams(
            collective_id=0, has_side_effects=True, vmem_limit_bytes=56 << 20
        ),
    )(patches, region.T, cell.T, *weights)


def solution(mesh):
    placed = (
        P("region", "chan"),
        P("region", None),
        P("region", None),
        P(None, "chan", None),
        P(None, "chan", None),
        P(None, "chan", None),
        P(),
        P(),
    )
    return jax.shard_map(
        shards, mesh=mesh, in_specs=placed, out_specs=P("chan", "region", None), check_vma=False
    )
```

```python
import jax
import jax.numpy as jnp
from jax import lax
from jax.experimental import pallas as pl
from jax.experimental.pallas import tpu as pltpu
from jax.sharding import PartitionSpec as P

C0 = 64
C1 = 128
C2 = 256
W = 128
HALF = 16
F32 = jnp.float32
BF16 = jnp.bfloat16
MESH = pl.DeviceIdType.MESH

PARTS = (((0, 1, 2), (6, 3, 2)), ((1, 2, 0), (5, 3, 3)), ((2, 0, 1), (5, 2, 3)))
STEPS = (2, 1, 3)


def jobs():
    chunks, start = [], 0
    for h in range(3):
        chunks.append([])
        for p, (_, sizes) in enumerate(PARTS):
            chunks[h].append((p, W * start, W * (start + sizes[h])))
            start += sizes[h]
    return chunks


def iota(shape, axis):
    return lax.broadcasted_iota(jnp.int32, shape, axis)


def shift(x, step):
    lane = iota(x.shape, 1)
    keep = lane < W - step if step > 0 else lane >= -step
    return jnp.where(keep, pltpu.roll(x, (-step) % W, 1), jnp.zeros_like(x))


def silu(v):
    h = 0.5 * v
    return h + h * jnp.tanh(h)


def swap_granules(x):
    rows = x.shape[0]
    row, gran = iota(x.shape, 0), iota(x.shape, 1) // 16
    for s in (1, 2, 4):
        down = pltpu.roll(pltpu.roll(x, 16 * s, 1), rows - s, 0)
        up = pltpu.roll(pltpu.roll(x, W - 16 * s, 1), s, 0)
        row_bit, gran_bit = (row & s) != 0, (gran & s) != 0
        x = jnp.where(row_bit == gran_bit, x, jnp.where(gran_bit, down, up))
    return x


def kernel(
    patches_ref, region_ref, cell_ref, wf_ref, wd_ref, wp_ref, wm_ref, wo_ref,
    out_ref,
    gathered, slots_out, slots_in, sums_out, sums_in, sums_own, tables_out, tables_in, codes_out, codes_in,
    wf_raw, wd_raw, wp_raw, wm_raw, wo_raw,
    wf, wd, wp, wm, wo,
    select, place, grid_f, tile, halo, im1, im2, imd, im4, out_b,
    load, t_send, t_recv, c_send, c_recv, route_send, route_recv,
    w_send, w_recv, x_send, x_recv, h_send, h_recv, o_send, o_recv,
):
    r, c = lax.axis_index("region"), lax.axis_index("chan")
    at = (r // 16, (r // 4) % 4, r % 4)
    other = 1 - c

    def along(axis, step):
        z, y, x = ((at[a] + step) % 4 if a == axis else at[a] for a in range(3))
        return (z * 16 + y * 4 + x, c)

    def remote(src, dst, send, recv, device):
        return pltpu.make_async_remote_copy(
            src_ref=src, dst_ref=dst, send_sem=send, recv_sem=recv,
            device_id=device, device_id_type=MESH,
        )

    def greet(device):
        pl.semaphore_signal(barrier, inc=1, device_id=device, device_id_type=MESH)

    barrier = pltpu.get_barrier_semaphore()
    for axis in range(3):
        for step in STEPS:
            greet(along(axis, step))
    greet((r, other))

    encoder = [(wf_ref, wf_raw.at[c]), (wd_ref, wd_raw.at[c]), (wp_ref, wp_raw.at[c])]
    loads = [
        pltpu.make_async_copy(src, dst, load.at[n])
        for n, (src, dst) in enumerate(
            [(patches_ref, gathered.at[0])] + encoder + [(wm_ref, wm_raw), (wo_ref, wo_raw)]
        )
    ]
    for copy in loads:
        copy.start()

    earlier = (iota((64, 64), 0) < iota((64, 64), 1)).astype(F32).astype(BF16)
    before = jnp.zeros((64, 1), F32)
    entry = jnp.zeros((8, 64), F32)
    for t in range(2):
        target = region_ref[t : t + 1, :]
        hit = jnp.where(iota((64, 64), 0) == target, 1.0, 0.0)
        count = jnp.dot(hit.astype(BF16), earlier, preferred_element_type=F32) + before
        before = before + jnp.sum(hit, axis=1, keepdims=True)
        rank = jnp.sum(hit * count, axis=0, keepdims=True)
        entry = jnp.where(iota((8, 64), 0) == t, target.astype(F32) * 4.0 + rank, entry)
        entry = jnp.where(
            iota((8, 64), 0) == t + 2, cell_ref[t : t + 1, :].astype(F32), entry
        )
    twice = (iota((64, W), 1) % 64 == iota((64, W), 0)).astype(F32).astype(BF16)
    tables_out[...] = jnp.dot(entry.astype(BF16), twice, preferred_element_type=F32)

    chunks = jobs()
    loads[0].wait()
    pl.semaphore_wait(barrier, 10)
    for axis in range(3):
        for step in STEPS:
            remote(
                tables_out, tables_in.at[axis, step], t_send, t_recv.at[axis], along(axis, step)
            ).start()
        tables_in[axis, 0] = tables_out[...]

    def spread_out(phase, h, src, dst):
        for step in STEPS:
            for p, a, b in chunks[h]:
                lanes = pl.ds(a, b - a)
                remote(
                    src(step).at[:, lanes], dst.at[step, :, lanes],
                    route_send.at[phase], route_recv.at[phase, h, p],
                    along(PARTS[p][0][phase], step),
                ).start()

    def arrive(phase, h, p, a, b, dst):
        whole = dst.at[pl.ds(1, 3), :, pl.ds(a, b - a)]
        remote(whole, whole, route_send.at[phase], route_recv.at[phase, h, p], (r, other)).wait_recv()

    for h in range(3):
        spread_out(0, h, lambda step: gathered.at[0], gathered)

    weight_copies = [
        remote(src, dst, w_send.at[n], w_recv.at[n], (r, other)) for n, (src, dst) in enumerate(encoder)
    ]
    for copy in weight_copies:
        copy.start()
    for copy in loads[1:]:
        copy.wait()
    for copy in weight_copies:
        copy.wait_recv()
    taps_from = [k + other * (6 - 6 * (k // 3)) for k in range(9)]
    for core in range(2):
        wf[64 * core : 64 * core + 64, :] = jnp.concatenate(
            [wf_raw[core, k] for k in taps_from], axis=1
        )
    for k, source in enumerate(taps_from):
        i, j = k // 3, k % 3
        for core in range(2):
            wd[128 * core : 128 * core + 128, 128 * k : 128 * k + 128] = wd_raw[core, source]
            wp[128 * core : 128 * core + 128, 256 * k : 256 * k + 256] = wp_raw[core, source]
        wm[:, 1152 * i + 128 * j : 1152 * i + 128 * j + 128] = wm_raw[source, :, :C1]
        wm[:, 1152 * i + 384 + 256 * j : 1152 * i + 384 + 256 * j + 256] = wm_raw[source, :, C1:]
        wo[:, 128 * k : 128 * k + 128] = wo_raw[source]

    lane = iota((8, W), 1)
    left = lane < 64
    for p, (axes, _) in enumerate(PARTS):
        here, second, third = axes
        three = tables_in.at[here, pl.ds(1, 3)]
        remote(three, three, t_send, t_recv.at[here], (r, other)).wait_recv()
        values = jnp.zeros((8, 256), F32)
        for half in range(2):
            table = jnp.where(left, tables_in[here, 2 * half], tables_in[here, 2 * half + 1])
            code = table.astype(jnp.int32)
            region = code // 4
            place_of = (region // 16, (region // 4) % 4, region % 4)
            slot = (
                ((place_of[second] - at[second]) & 3) * 64
                + (2 * half + lane // 64) * 16
                + ((place_of[third] - at[third]) & 3) * 4
                + code % 4
            )
            slot = jnp.where(place_of[here] == at[here], slot, -1)
            hits = [iota((256, W), 0) == slot[t : t + 1] for t in range(2)]
            select[p, :, W * half : W * half + W] = (
                jnp.where(jnp.logical_or(hits[0], hits[1]), 1.0, 0.0).astype(BF16)
            )
            for t in range(2):
                cells = jnp.broadcast_to(table[t + 2 : t + 3] + 1.0, (8, W)).astype(BF16)
                values = values + lax.dot_general(
                    cells, jnp.where(hits[t], 1.0, 0.0).astype(BF16),
                    (((1,), (1,)), ((), ())), preferred_element_type=F32,
                )
        for step in range(4):
            value = values[:, W * (step // 2) : W * (step // 2) + W]
            turned = pltpu.roll(value, 64, 1)
            value = jnp.where(left, value, turned) if step % 2 == 0 else jnp.where(left, turned, value)
            value = jnp.where(value > 0.0, value - 1.0 + (32 * ((lane // 4) % 4)).astype(F32), -1.0)
            if step == 0:
                codes_in[p, 0] = value
            else:
                codes_out[p, step] = value
        for step in STEPS:
            remote(
                codes_out.at[p, step], codes_in.at[p, step], c_send, c_recv.at[p], along(second, step)
            ).start()

    for h in range(3):
        for p, a, b in chunks[h]:
            arrive(0, h, p, a, b, gathered)
            for n in range(a, b, 256):
                e = min(n + 256, b)
                slots = jnp.dot(
                    select[p], gathered[:, :, n:e].reshape(256, e - n), preferred_element_type=F32
                ).astype(BF16)
                slots_in[0, :, n:e] = slots[:64]
                slots_out[:, :, n:e] = slots[64:].reshape(3, 64, e - n)
        spread_out(1, h, lambda step: slots_out.at[step - 1], slots_in)

    for p in range(3):
        three = codes_in.at[p, pl.ds(1, 3)]
        remote(three, three, c_send, c_recv.at[p], (r, other)).wait_recv()
        for half in range(2):
            code = jnp.where(left, codes_in[p, 2 * half], codes_in[p, 2 * half + 1])[0:1]
            place[p, :, W * half : W * half + W] = jnp.where(
                iota((W, W), 0).astype(F32) == code, 1.0, 0.0
            ).astype(BF16)
    for h in range(3):
        for p, a, b in chunks[h]:
            arrive(1, h, p, a, b, slots_in)
            for n in range(a, b, 256):
                e = min(n + 256, b)
                sums = jnp.dot(
                    place[p], slots_in[:, :, n:e].reshape(256, e - n), preferred_element_type=F32
                )
                sums_own[:, n:e] = sums[:32]
                sums_out[:, :, n:e] = sums[32:].astype(BF16).reshape(3, 32, e - n)
        spread_out(2, h, lambda step: sums_out.at[step - 1], sums_in)

    border = jnp.logical_or(jnp.logical_and(r == 0, c == 0), jnp.logical_and(r == 63, c == 1))
    keep = jnp.where(border, 0.0, 1.0)

    def tile_row(v):
        return (15 - v) * other + (16 + v) * c

    even = iota((C2, W), 1) % 2 == 0

    def taps(x):
        return shift(x, -1), x, shift(x, 1)

    def settle(e):
        mine = pl.ds(pl.multiple_of(32 * c + 16 * e, 16), 16)
        tile[:, mine, :] = grid_f[e].astype(BF16).reshape(32, 16, W)
        copy = remote(tile.at[:, mine], tile.at[:, mine], x_send.at[e], x_recv.at[e], (r, other))
        copy.start()
        return copy

    def halo_copies(e, core):
        rows = pl.ds(pl.multiple_of(32 * core + 16 * e, 16), 16)
        for to in range(2):
            yield remote(
                tile.at[pl.ds(26 * (1 - to), 6), rows], halo.at[:, rows],
                h_send.at[e, to], h_recv.at[e, core], ((r + 1 + 62 * to) % 64, to),
            )

    def send_halo(e):
        for copy in halo_copies(e, c):
            copy.start()

    def widen(e, core):
        channels = pl.multiple_of(32 * core + 16 * e, 16)
        for l in range(22):
            for j, tap in enumerate(taps(tile[tile_row(l - 6), pl.ds(channels, 16), :])):
                im1[l, pl.ds(C0 * j + channels, 16), :] = tap

    tile_copies = []
    for h in range(3):
        for p, a, b in chunks[h]:
            arrive(2, h, p, a, b, sums_in)
            total = sums_own[:, a:b]
            for step in STEPS:
                total = total + sums_in[step, :, a:b].astype(F32)
            for n in range(a, b, W):
                block = swap_granules(total[:, n - a : n - a + W])
                e, ch = n // W // 16, n // W % 16
                for band in range(4):
                    grid_f[e, pl.ds(W * band + ch, 8, stride=16), :] = block[8 * band : 8 * band + 8]
        if h != 1:
            e = h // 2
            tile_copies.append(settle(e))
            if e == 1:
                send_halo(e)
            widen(e, c)
            tile_copies[e].wait_recv()
            if e == 0:
                send_halo(e)
            widen(e, other)

    def first_rows_of(n):
        f = 4 * n
        window = jnp.concatenate(
            [im1[f + t : f + t + 3].reshape(576, W) for t in range(4)], axis=1
        )
        total = jnp.dot(wf[...], window, preferred_element_type=F32)
        for t in range(4):
            row = silu(total[:, W * t : W * t + W])
            if f + t >= 21:
                row = row * keep
            for j, tap in enumerate(taps(row.astype(BF16))):
                im2[f + t, C1 * j : C1 * j + C1] = tap

    def spread_pair(at_pair, x):
        for j, tap in enumerate((shift(x, -2), x, shift(x, 2))):
            imd[at_pair, C2 * j : C2 * j + C2] = tap

    def second_pair(m):
        window = jnp.concatenate(
            [
                jnp.concatenate([im2[4 * m + 2 * t + i + other, 0:384] for i in range(3)], axis=0)
                for t in range(2)
            ],
            axis=1,
        )
        total = jnp.dot(wd[...], window, preferred_element_type=F32)
        pair = silu(jnp.where(even, total[:, :W], pltpu.roll(total[:, W:], 1, 1)))
        if m == 5:
            pair = pair * keep
        spread_pair(2 * m, pair.astype(BF16))

    def blend(m):
        a, b = imd[2 * m, C2 : 2 * C2], imd[2 * m + 2, C2 : 2 * C2]
        spread_pair(2 * m + 1, jnp.where(even, shift(a, 1), shift(b, -1)))

    def third_pairs(ms):
        window = jnp.concatenate([imd[2 * m : 2 * m + 3].reshape(2304, W) for m in ms], axis=1)
        total = jnp.dot(wp[...], window, preferred_element_type=F32)
        for t, m in enumerate(ms):
            third = silu(total[:, W * t : W * t + W]) + imd[2 * m + 1, C2 : 2 * C2].astype(F32)
            if m == 4:
                third = jnp.where(even, third, third * keep)
            third = third.astype(BF16)
            l1, l2, r1, r2 = shift(third, -1), shift(third, -2), shift(third, 1), shift(third, 2)
            lane = iota((C2, W), 1)
            zero = jnp.zeros_like(third)
            ups = (
                (
                    jnp.where(even, l2, l1),
                    jnp.where(even, third, l1),
                    jnp.where(lane == W - 1, zero, jnp.where(even, third, r1)),
                ),
                (
                    jnp.where(lane == 0, zero, jnp.where(even, l1, third)),
                    jnp.where(even, r1, third),
                    jnp.where(even, r1, r2),
                ),
            )
            for half in range(2):
                for j in range(3):
                    f = 4 * m + 3 + 2 * half
                    im2[f, 384 + C2 * j : 384 + C2 * j + C2] = ups[half][j]
                    im2[f + 1, 384 + C2 * j : 384 + C2 * j + C2] = ups[half][j]

    def fourth_rows(n):
        g = 2 * n
        window = jnp.concatenate(
            [im2[g + 3 + t : g + 6 + t].reshape(3456, W) for t in range(2)], axis=1
        )
        total = jnp.dot(wm[...], window, preferred_element_type=F32)
        for t in range(2):
            row = silu(total[:, W * t : W * t + W])
            if g + t == 17:
                row = row * keep
            for j, tap in enumerate(taps(row.astype(BF16))):
                im4[g + t, C1 * j : C1 * j + C1] = tap

    def out_rows(n):
        f = 4 * n
        window = jnp.concatenate(
            [im4[f + t : f + t + 3].reshape(1152, W) for t in range(4)], axis=1
        )
        total = jnp.dot(wo[...], window, preferred_element_type=F32)
        for t in range(4):
            at_row = tile_row(f + t)
            row = total[:, W * t : W * t + W] + tile[at_row].astype(F32)
            out_b[f + t] = row.astype(BF16)
            remote(
                out_b.at[f + t, pl.ds(pl.multiple_of(32 * other, 32), 32)], out_ref.at[at_row],
                o_send, o_recv, (r, other),
            ).start()
            out_ref[at_row] = out_b[f + t, pl.ds(pl.multiple_of(32 * c, 32), 32), :]

    for n in range(5):
        first_rows_of(n)
    for m in range(4):
        second_pair(m)
    for m in range(3):
        blend(m)
    third_pairs([0, 1])
    third_pairs([2])
    for e in range(2):
        for core in range(2):
            next(halo_copies(e, core)).wait_recv()

    @pl.when(border)
    def _():
        halo[...] = jnp.zeros((6, C0, W), BF16)

    for l in range(6):
        for j, tap in enumerate(taps(halo[(5 - l) * other + l * c])):
            im1[22 + l, C0 * j : C0 * j + C0] = tap
    for n in range(5, 7):
        first_rows_of(n)
    for m in range(4, 6):
        second_pair(m)
    for m in range(3, 5):
        blend(m)
    third_pairs([3, 4])
    for n in range(9):
        fourth_rows(n)
    for n in range(4):
        out_rows(n)
    for copy in weight_copies + tile_copies + [*halo_copies(0, c), *halo_copies(1, c)]:
        copy.wait_send()
    for phase, buffer in enumerate((gathered, slots_in, sums_in)):
        whole = buffer.at[pl.ds(1, 3)]
        remote(whole, whole, route_send.at[phase], o_recv, (r, other)).wait_send()
    three = tables_in.at[:, pl.ds(1, 3)]
    remote(three, three, t_send, o_recv, (r, other)).wait_send()
    three = codes_in.at[:, pl.ds(1, 3)]
    remote(three, three, c_send, o_recv, (r, other)).wait_send()
    rows = out_ref.at[pl.ds(0, HALF)]
    remote(rows, rows, o_send, o_recv, (r, other)).wait()


def shards(patches, region, cell, *weights):
    vmem = pl.BlockSpec(memory_space=pltpu.VMEM)
    anywhere = pl.BlockSpec(memory_space=pl.ANY)
    dma = pltpu.SemaphoreType.DMA
    rows = pl.pallas_call(
        kernel,
        out_shape=jax.ShapeDtypeStruct((32, 32, W), BF16),
        in_specs=[anywhere, vmem, vmem] + [anywhere] * 5,
        out_specs=vmem,
        scratch_shapes=[
            pltpu.VMEM((4, 64, 4096), BF16),
            pltpu.VMEM((3, 64, 4096), BF16),
            pltpu.VMEM((4, 64, 4096), BF16),
            pltpu.VMEM((3, 32, 4096), BF16),
            pltpu.VMEM((4, 32, 4096), BF16),
            pltpu.VMEM((32, 4096), F32),
            pltpu.VMEM((8, W), F32),
            pltpu.VMEM((3, 4, 8, W), F32),
            pltpu.VMEM((3, 4, 8, W), F32),
            pltpu.VMEM((3, 4, 8, W), F32),
            pltpu.VMEM((2, 9, 64, C0), BF16),
            pltpu.VMEM((2, 9, 128, C1), BF16),
            pltpu.VMEM((2, 9, 128, C2), BF16),
            pltpu.VMEM((9, C1, C1 + C2), BF16),
            pltpu.VMEM((9, C0, C1), BF16),
            pltpu.VMEM((C1, 9 * C0), BF16),
            pltpu.VMEM((C2, 9 * C1), BF16),
            pltpu.VMEM((C2, 9 * C2), BF16),
            pltpu.VMEM((C1, 9 * (C1 + C2)), BF16),
            pltpu.VMEM((C0, 9 * C1), BF16),
            pltpu.VMEM((3, 256, 256), BF16),
            pltpu.VMEM((3, W, 256), BF16),
            pltpu.VMEM((2, 512, W), F32),
            pltpu.VMEM((32, C0, W), BF16),
            pltpu.VMEM((6, C0, W), BF16),
            pltpu.VMEM((30, 3 * C0, W), BF16),
            pltpu.VMEM((28, 3 * (C1 + C2), W), BF16),
            pltpu.VMEM((11, 3 * C2, W), BF16),
            pltpu.VMEM((18, 3 * C1, W), BF16),
            pltpu.VMEM((HALF, C0, W), BF16),
            dma((6,)), dma, dma((3,)), dma, dma((3,)), dma((3,)), dma((3, 3, 3)),
            dma((3,)), dma((3,)), dma((2,)), dma((2,)), dma((2, 2)), dma((2, 2)), dma, dma,
        ],
        compiler_params=pltpu.CompilerParams(
            collective_id=0, has_side_effects=True, vmem_limit_bytes=56 << 20
        ),
    )(patches, region.T, cell.T, *weights)
    return jnp.transpose(rows, (1, 0, 2))


def solution(mesh):
    placed = (
        P("region", "chan"),
        P("region", None),
        P("region", None),
        P(None, "chan", None),
        P(None, "chan", None),
        P(None, "chan", None),
        P(),
        P(),
    )
    return jax.shard_map(
        shards, mesh=mesh, in_specs=placed, out_specs=P("chan", "region", None), check_vma=False
    )
```

```python
import jax
import jax.numpy as jnp
from jax import lax
from jax.experimental import pallas as pl
from jax.experimental.pallas import tpu as pltpu
from jax.sharding import PartitionSpec as P

C0 = 64
C1 = 128
C2 = 256
W = 128
HALF = 16
F32 = jnp.float32
BF16 = jnp.bfloat16
MESH = pl.DeviceIdType.MESH

PARTS = (((0, 1, 2), (6, 3, 2)), ((1, 2, 0), (5, 3, 3)), ((2, 0, 1), (5, 2, 3)))
STEPS = (2, 1, 3)


def jobs():
    chunks, start = [], 0
    for h in range(3):
        chunks.append([])
        for p, (_, sizes) in enumerate(PARTS):
            chunks[h].append((p, W * start, W * (start + sizes[h])))
            start += sizes[h]
    return chunks


def iota(shape, axis):
    return lax.broadcasted_iota(jnp.int32, shape, axis)


def shift(x, step):
    lane = iota(x.shape, 1)
    keep = lane < W - step if step > 0 else lane >= -step
    return jnp.where(keep, pltpu.roll(x, (-step) % W, 1), jnp.zeros_like(x))


def silu(v):
    h = 0.5 * v
    return h + h * jnp.tanh(h)


def swap_granules(x):
    rows = x.shape[0]
    row, gran = iota(x.shape, 0), iota(x.shape, 1) // 16
    for s in (1, 2, 4):
        down = pltpu.roll(pltpu.roll(x, 16 * s, 1), rows - s, 0)
        up = pltpu.roll(pltpu.roll(x, W - 16 * s, 1), s, 0)
        row_bit, gran_bit = (row & s) != 0, (gran & s) != 0
        x = jnp.where(row_bit == gran_bit, x, jnp.where(gran_bit, down, up))
    return x


def kernel(
    patches_ref, region_ref, cell_ref, wf_ref, wd_ref, wp_ref, wm_ref, wo_ref,
    out_ref,
    gathered, slots_out, slots_in, sums_out, sums_in, sums_own, tables_out, tables_in, codes_out, codes_in,
    wf_raw, wd_raw, wp_raw, wm_raw, wo_raw,
    wf, wd, wp, wm, wo,
    select, place, grid_f, tile, halo, im1, im2, imd, im4, out_b,
    load, t_send, t_recv, c_send, c_recv, route_send, route_recv,
    w_send, w_recv, x_send, x_recv, h_send, h_recv, o_send, o_recv, o_own,
):
    r, c = lax.axis_index("region"), lax.axis_index("chan")
    at = (r // 16, (r // 4) % 4, r % 4)
    other = 1 - c

    def along(axis, step):
        z, y, x = ((at[a] + step) % 4 if a == axis else at[a] for a in range(3))
        return (z * 16 + y * 4 + x, c)

    def remote(src, dst, send, recv, device):
        return pltpu.make_async_remote_copy(
            src_ref=src, dst_ref=dst, send_sem=send, recv_sem=recv,
            device_id=device, device_id_type=MESH,
        )

    def greet(device):
        pl.semaphore_signal(barrier, inc=1, device_id=device, device_id_type=MESH)

    barrier = pltpu.get_barrier_semaphore()
    for axis in range(3):
        for step in STEPS:
            greet(along(axis, step))
    greet((r, other))

    encoder = [(wf_ref, wf_raw.at[c]), (wd_ref, wd_raw.at[c]), (wp_ref, wp_raw.at[c])]
    loads = [
        pltpu.make_async_copy(src, dst, load.at[n])
        for n, (src, dst) in enumerate(
            [(patches_ref, gathered.at[0])] + encoder + [(wm_ref, wm_raw), (wo_ref, wo_raw)]
        )
    ]
    for copy in loads:
        copy.start()

    earlier = (iota((64, 64), 0) < iota((64, 64), 1)).astype(F32).astype(BF16)
    before = jnp.zeros((64, 1), F32)
    entry = jnp.zeros((8, 64), F32)
    for t in range(2):
        target = region_ref[t : t + 1, :]
        hit = jnp.where(iota((64, 64), 0) == target, 1.0, 0.0)
        count = jnp.dot(hit.astype(BF16), earlier, preferred_element_type=F32) + before
        before = before + jnp.sum(hit, axis=1, keepdims=True)
        rank = jnp.sum(hit * count, axis=0, keepdims=True)
        entry = jnp.where(iota((8, 64), 0) == t, target.astype(F32) * 4.0 + rank, entry)
        entry = jnp.where(
            iota((8, 64), 0) == t + 2, cell_ref[t : t + 1, :].astype(F32), entry
        )
    twice = (iota((64, W), 1) % 64 == iota((64, W), 0)).astype(F32).astype(BF16)
    tables_out[...] = jnp.dot(entry.astype(BF16), twice, preferred_element_type=F32)

    chunks = jobs()
    loads[0].wait()
    pl.semaphore_wait(barrier, 10)
    for axis in range(3):
        for step in STEPS:
            remote(
                tables_out, tables_in.at[axis, step], t_send, t_recv.at[axis], along(axis, step)
            ).start()
        tables_in[axis, 0] = tables_out[...]

    def spread_out(phase, h, src, dst):
        for step in STEPS:
            for p, a, b in chunks[h]:
                lanes = pl.ds(a, b - a)
                remote(
                    src(step).at[:, lanes], dst.at[step, :, lanes],
                    route_send.at[phase], route_recv.at[phase, h, p],
                    along(PARTS[p][0][phase], step),
                ).start()

    def arrive(phase, h, p, a, b, dst):
        whole = dst.at[pl.ds(1, 3), :, pl.ds(a, b - a)]
        remote(whole, whole, route_send.at[phase], route_recv.at[phase, h, p], (r, other)).wait_recv()

    for h in range(3):
        spread_out(0, h, lambda step: gathered.at[0], gathered)

    weight_copies = [
        remote(src, dst, w_send.at[n], w_recv.at[n], (r, other)) for n, (src, dst) in enumerate(encoder)
    ]
    for copy in weight_copies:
        copy.start()
    for copy in loads[1:]:
        copy.wait()
    for copy in weight_copies:
        copy.wait_recv()
    taps_from = [k + other * (6 - 6 * (k // 3)) for k in range(9)]
    for core in range(2):
        wf[64 * core : 64 * core + 64, :] = jnp.concatenate(
            [wf_raw[core, k] for k in taps_from], axis=1
        )
    for k, source in enumerate(taps_from):
        i, j = k // 3, k % 3
        for core in range(2):
            wp[128 * core : 128 * core + 128, 256 * k : 256 * k + 256] = wp_raw[core, source]
        wm[:, 1152 * i + 128 * j : 1152 * i + 128 * j + 128] = wm_raw[source, :, :C1]
        wm[:, 1152 * i + 384 + 256 * j : 1152 * i + 384 + 256 * j + 256] = wm_raw[source, :, C1:]
        wo[:, 128 * k : 128 * k + 128] = wo_raw[source]

    for k in range(12):
        i, j = k // 3, k % 3
        source = 3 * (min(3 - i, 2) * other + min(i, 2) * c) + j
        used = (c == 1 if i == 0 else c == 0) if i in (0, 3) else None
        for core in range(2):
            value = wd_raw[core, source]
            if used is not None:
                value = jnp.where(used, value, jnp.zeros_like(value))
            wd[128 * core : 128 * core + 128, 128 * k : 128 * k + 128] = value

    lane = iota((8, W), 1)
    left = lane < 64
    for p, (axes, _) in enumerate(PARTS):
        here, second, third = axes
        three = tables_in.at[here, pl.ds(1, 3)]
        remote(three, three, t_send, t_recv.at[here], (r, other)).wait_recv()
        values = jnp.zeros((8, 256), F32)
        for half in range(2):
            table = jnp.where(left, tables_in[here, 2 * half], tables_in[here, 2 * half + 1])
            code = table.astype(jnp.int32)
            region = code // 4
            place_of = (region // 16, (region // 4) % 4, region % 4)
            slot = (
                ((place_of[second] - at[second]) & 3) * 64
                + (2 * half + lane // 64) * 16
                + ((place_of[third] - at[third]) & 3) * 4
                + code % 4
            )
            slot = jnp.where(place_of[here] == at[here], slot, -1)
            hits = [iota((256, W), 0) == slot[t : t + 1] for t in range(2)]
            select[p, :, W * half : W * half + W] = (
                jnp.where(jnp.logical_or(hits[0], hits[1]), 1.0, 0.0).astype(BF16)
            )
            for t in range(2):
                cells = jnp.broadcast_to(table[t + 2 : t + 3] + 1.0, (8, W)).astype(BF16)
                values = values + lax.dot_general(
                    cells, jnp.where(hits[t], 1.0, 0.0).astype(BF16),
                    (((1,), (1,)), ((), ())), preferred_element_type=F32,
                )
        for step in range(4):
            value = values[:, W * (step // 2) : W * (step // 2) + W]
            turned = pltpu.roll(value, 64, 1)
            value = jnp.where(left, value, turned) if step % 2 == 0 else jnp.where(left, turned, value)
            value = jnp.where(value > 0.0, value - 1.0 + (32 * ((lane // 4) % 4)).astype(F32), -1.0)
            if step == 0:
                codes_in[p, 0] = value
            else:
                codes_out[p, step] = value
        for step in STEPS:
            remote(
                codes_out.at[p, step], codes_in.at[p, step], c_send, c_recv.at[p], along(second, step)
            ).start()

    for h in range(3):
        for p, a, b in chunks[h]:
            arrive(0, h, p, a, b, gathered)
            for n in range(a, b, 256):
                e = min(n + 256, b)
                slots = jnp.dot(
                    select[p], gathered[:, :, n:e].reshape(256, e - n), preferred_element_type=F32
                ).astype(BF16)
                slots_in[0, :, n:e] = slots[:64]
                slots_out[:, :, n:e] = slots[64:].reshape(3, 64, e - n)
        spread_out(1, h, lambda step: slots_out.at[step - 1], slots_in)

    for p in range(3):
        three = codes_in.at[p, pl.ds(1, 3)]
        remote(three, three, c_send, c_recv.at[p], (r, other)).wait_recv()
        for half in range(2):
            code = jnp.where(left, codes_in[p, 2 * half], codes_in[p, 2 * half + 1])[0:1]
            place[p, :, W * half : W * half + W] = jnp.where(
                iota((W, W), 0).astype(F32) == code, 1.0, 0.0
            ).astype(BF16)
    for h in range(3):
        for p, a, b in chunks[h]:
            arrive(1, h, p, a, b, slots_in)
            for n in range(a, b, 256):
                e = min(n + 256, b)
                sums = jnp.dot(
                    place[p], slots_in[:, :, n:e].reshape(256, e - n), preferred_element_type=F32
                )
                sums_own[:, n:e] = sums[:32]
                sums_out[:, :, n:e] = sums[32:].astype(BF16).reshape(3, 32, e - n)
        spread_out(2, h, lambda step: sums_out.at[step - 1], sums_in)

    border = jnp.logical_or(jnp.logical_and(r == 0, c == 0), jnp.logical_and(r == 63, c == 1))
    keep = jnp.where(border, 0.0, 1.0)

    def tile_row(v):
        return (15 - v) * other + (16 + v) * c

    even = iota((C2, W), 1) % 2 == 0

    def taps(x):
        return shift(x, -1), x, shift(x, 1)

    def settle(e):
        mine = pl.ds(pl.multiple_of(32 * c + 16 * e, 16), 16)
        tile[:, mine, :] = grid_f[e].astype(BF16).reshape(32, 16, W)
        copy = remote(tile.at[:, mine], tile.at[:, mine], x_send.at[e], x_recv.at[e], (r, other))
        copy.start()
        return copy

    def halo_copies(e, core):
        rows = pl.ds(pl.multiple_of(32 * core + 16 * e, 16), 16)
        for to in range(2):
            yield remote(
                tile.at[pl.ds(26 * (1 - to), 6), rows], halo.at[:, rows],
                h_send.at[e, to], h_recv.at[e, core], ((r + 1 + 62 * to) % 64, to),
            )

    def send_halo(e):
        for copy in halo_copies(e, c):
            copy.start()

    def widen(e, core):
        channels = pl.multiple_of(32 * core + 16 * e, 16)
        for l in range(22):
            for j, tap in enumerate(taps(tile[tile_row(l - 6), pl.ds(channels, 16), :])):
                im1[l, pl.ds(C0 * j + channels, 16), :] = tap

    tile_copies = []
    for h in range(3):
        for p, a, b in chunks[h]:
            arrive(2, h, p, a, b, sums_in)
            total = sums_own[:, a:b]
            for step in STEPS:
                total = total + sums_in[step, :, a:b].astype(F32)
            for n in range(a, b, W):
                block = swap_granules(total[:, n - a : n - a + W])
                e, ch = n // W // 16, n // W % 16
                for band in range(4):
                    grid_f[e, pl.ds(W * band + ch, 8, stride=16), :] = block[8 * band : 8 * band + 8]
        if h != 1:
            e = h // 2
            tile_copies.append(settle(e))
            if e == 1:
                send_halo(e)
            widen(e, c)
            tile_copies[e].wait_recv()
            if e == 0:
                send_halo(e)
            widen(e, other)

    def first_rows_of(n):
        f = 4 * n
        window = jnp.concatenate(
            [im1[f + t : f + t + 3].reshape(576, W) for t in range(4)], axis=1
        )
        total = jnp.dot(wf[...], window, preferred_element_type=F32)
        for t in range(4):
            row = silu(total[:, W * t : W * t + W])
            if f + t >= 21:
                row = row * keep
            for j, tap in enumerate(taps(row.astype(BF16))):
                im2[f + t, C1 * j : C1 * j + C1] = tap

    def spread_pair(at_pair, x):
        for j, tap in enumerate((shift(x, -2), x, shift(x, 2))):
            imd[at_pair, C2 * j : C2 * j + C2] = tap

    def second_pair(m):
        window = jnp.concatenate(
            [
                jnp.concatenate([im2[4 * m + 2 * t + i, 0:384] for i in range(4)], axis=0)
                for t in range(2)
            ],
            axis=1,
        )
        total = jnp.dot(wd[...], window, preferred_element_type=F32)
        pair = silu(jnp.where(even, total[:, :W], pltpu.roll(total[:, W:], 1, 1)))
        if m == 5:
            pair = pair * keep
        spread_pair(2 * m, pair.astype(BF16))

    def blend(m):
        a, b = imd[2 * m, C2 : 2 * C2], imd[2 * m + 2, C2 : 2 * C2]
        spread_pair(2 * m + 1, jnp.where(even, shift(a, 1), shift(b, -1)))

    def third_pairs(ms):
        window = jnp.concatenate([imd[2 * m : 2 * m + 3].reshape(2304, W) for m in ms], axis=1)
        total = jnp.dot(wp[...], window, preferred_element_type=F32)
        for t, m in enumerate(ms):
            third = silu(total[:, W * t : W * t + W]) + imd[2 * m + 1, C2 : 2 * C2].astype(F32)
            if m == 4:
                third = jnp.where(even, third, third * keep)
            third = third.astype(BF16)
            l1, l2, r1, r2 = shift(third, -1), shift(third, -2), shift(third, 1), shift(third, 2)
            lane = iota((C2, W), 1)
            zero = jnp.zeros_like(third)
            ups = (
                (
                    jnp.where(even, l2, l1),
                    jnp.where(even, third, l1),
                    jnp.where(lane == W - 1, zero, jnp.where(even, third, r1)),
                ),
                (
                    jnp.where(lane == 0, zero, jnp.where(even, l1, third)),
                    jnp.where(even, r1, third),
                    jnp.where(even, r1, r2),
                ),
            )
            for half in range(2):
                for j in range(3):
                    f = 4 * m + 3 + 2 * half
                    im2[f, 384 + C2 * j : 384 + C2 * j + C2] = ups[half][j]
                    im2[f + 1, 384 + C2 * j : 384 + C2 * j + C2] = ups[half][j]

    def fourth_rows(n):
        g = 2 * n
        window = jnp.concatenate(
            [im2[g + 3 + t : g + 6 + t].reshape(3456, W) for t in range(2)], axis=1
        )
        total = jnp.dot(wm[...], window, preferred_element_type=F32)
        for t in range(2):
            row = silu(total[:, W * t : W * t + W])
            if g + t == 17:
                row = row * keep
            for j, tap in enumerate(taps(row.astype(BF16))):
                im4[g + t, C1 * j : C1 * j + C1] = tap

    def out_rows(n):
        f = 4 * n
        window = jnp.concatenate(
            [im4[f + t : f + t + 3].reshape(1152, W) for t in range(4)], axis=1
        )
        total = jnp.dot(wo[...], window, preferred_element_type=F32)
        for t in range(4):
            row = total[:, W * t : W * t + W] + tile[tile_row(f + t)].astype(F32)
            out_b[(15 - f - t) * other + (f + t) * c] = row.astype(BF16)
        start = (12 - f) * other + f * c
        source, target = out_b.at[pl.ds(start, 4)], out_ref.at[pl.ds(HALF * c + start, 4)]
        remote(
            source.at[:, pl.ds(pl.multiple_of(32 * other, 32), 32)], target, o_send, o_recv, (r, other)
        ).start()
        pltpu.make_async_copy(
            source.at[:, pl.ds(pl.multiple_of(32 * c, 32), 32)], target, o_own
        ).start()

    for n in range(5):
        first_rows_of(n)
        if n:
            second_pair(n - 1)
        if n > 1:
            blend(n - 2)
        if n == 3:
            third_pairs([0, 1])
    third_pairs([2])
    for e in range(2):
        for core in range(2):
            next(halo_copies(e, core)).wait_recv()

    @pl.when(border)
    def _():
        halo[...] = jnp.zeros((6, C0, W), BF16)

    for l in range(6):
        for j, tap in enumerate(taps(halo[(5 - l) * other + l * c])):
            im1[22 + l, C0 * j : C0 * j + C0] = tap
    for n in range(5, 7):
        first_rows_of(n)
    for m in range(4, 6):
        second_pair(m)
    for m in range(3, 5):
        blend(m)
    third_pairs([3, 4])
    for n in range(9):
        fourth_rows(n)
    for n in range(4):
        out_rows(n)
    for copy in weight_copies + tile_copies + [*halo_copies(0, c), *halo_copies(1, c)]:
        copy.wait_send()
    for phase, buffer in enumerate((gathered, slots_in, sums_in)):
        whole = buffer.at[pl.ds(1, 3)]
        remote(whole, whole, route_send.at[phase], o_recv, (r, other)).wait_send()
    three = tables_in.at[:, pl.ds(1, 3)]
    remote(three, three, t_send, o_recv, (r, other)).wait_send()
    three = codes_in.at[:, pl.ds(1, 3)]
    remote(three, three, c_send, o_recv, (r, other)).wait_send()
    rows = out_ref.at[pl.ds(0, HALF)]
    remote(rows, rows, o_send, o_recv, (r, other)).wait()
    pltpu.make_async_copy(rows, rows, o_own).wait()


def shards(patches, region, cell, *weights):
    vmem = pl.BlockSpec(memory_space=pltpu.VMEM)
    anywhere = pl.BlockSpec(memory_space=pl.ANY)
    dma = pltpu.SemaphoreType.DMA
    rows = pl.pallas_call(
        kernel,
        out_shape=jax.ShapeDtypeStruct((32, 32, W), BF16),
        in_specs=[anywhere, vmem, vmem] + [anywhere] * 5,
        out_specs=anywhere,
        scratch_shapes=[
            pltpu.VMEM((4, 64, 4096), BF16),
            pltpu.VMEM((3, 64, 4096), BF16),
            pltpu.VMEM((4, 64, 4096), BF16),
            pltpu.VMEM((3, 32, 4096), BF16),
            pltpu.VMEM((4, 32, 4096), BF16),
            pltpu.VMEM((32, 4096), F32),
            pltpu.VMEM((8, W), F32),
            pltpu.VMEM((3, 4, 8, W), F32),
            pltpu.VMEM((3, 4, 8, W), F32),
            pltpu.VMEM((3, 4, 8, W), F32),
            pltpu.VMEM((2, 9, 64, C0), BF16),
            pltpu.VMEM((2, 9, 128, C1), BF16),
            pltpu.VMEM((2, 9, 128, C2), BF16),
            pltpu.VMEM((9, C1, C1 + C2), BF16),
            pltpu.VMEM((9, C0, C1), BF16),
            pltpu.VMEM((C1, 9 * C0), BF16),
            pltpu.VMEM((C2, 12 * C1), BF16),
            pltpu.VMEM((C2, 9 * C2), BF16),
            pltpu.VMEM((C1, 9 * (C1 + C2)), BF16),
            pltpu.VMEM((C0, 9 * C1), BF16),
            pltpu.VMEM((3, 256, 256), BF16),
            pltpu.VMEM((3, W, 256), BF16),
            pltpu.VMEM((2, 512, W), F32),
            pltpu.VMEM((32, C0, W), BF16),
            pltpu.VMEM((6, C0, W), BF16),
            pltpu.VMEM((30, 3 * C0, W), BF16),
            pltpu.VMEM((28, 3 * (C1 + C2), W), BF16),
            pltpu.VMEM((11, 3 * C2, W), BF16),
            pltpu.VMEM((18, 3 * C1, W), BF16),
            pltpu.VMEM((HALF, C0, W), BF16),
            dma((6,)), dma, dma((3,)), dma, dma((3,)), dma((3,)), dma((3, 3, 3)),
            dma((3,)), dma((3,)), dma((2,)), dma((2,)), dma((2, 2)), dma((2, 2)), dma, dma, dma,
        ],
        compiler_params=pltpu.CompilerParams(
            collective_id=0, has_side_effects=True, vmem_limit_bytes=56 << 20
        ),
    )(patches, region.T, cell.T, *weights)
    return jnp.transpose(rows, (1, 0, 2))


def solution(mesh):
    placed = (
        P("region", "chan"),
        P("region", None),
        P("region", None),
        P(None, "chan", None),
        P(None, "chan", None),
        P(None, "chan", None),
        P(),
        P(),
    )
    return jax.shard_map(
        shards, mesh=mesh, in_specs=placed, out_specs=P("chan", "region", None), check_vma=False
    )
```

```python
import jax
import jax.numpy as jnp
from jax import lax
from jax.experimental import pallas as pl
from jax.experimental.pallas import tpu as pltpu
from jax.sharding import PartitionSpec as P

C0 = 64
C1 = 128
C2 = 256
W = 128
HALF = 16
F32 = jnp.float32
BF16 = jnp.bfloat16
MESH = pl.DeviceIdType.MESH

PARTS = (((0, 1, 2), (6, 3, 2)), ((1, 2, 0), (5, 3, 3)), ((2, 0, 1), (5, 2, 3)))
STEPS = (2, 1, 3)


def jobs():
    chunks, start = [], 0
    for h in range(3):
        chunks.append([])
        for p, (_, sizes) in enumerate(PARTS):
            chunks[h].append((p, W * start, W * (start + sizes[h])))
            start += sizes[h]
    return chunks


def iota(shape, axis):
    return lax.broadcasted_iota(jnp.int32, shape, axis)


def shift(x, step):
    lane = iota(x.shape, 1)
    keep = lane < W - step if step > 0 else lane >= -step
    return jnp.where(keep, pltpu.roll(x, (-step) % W, 1), jnp.zeros_like(x))


def silu(v):
    h = 0.5 * v
    return h + h * jnp.tanh(h)


def swap_granules(x):
    rows = x.shape[0]
    row, gran = iota(x.shape, 0), iota(x.shape, 1) // 16
    for s in (1, 2, 4):
        down = pltpu.roll(pltpu.roll(x, 16 * s, 1), rows - s, 0)
        up = pltpu.roll(pltpu.roll(x, W - 16 * s, 1), s, 0)
        row_bit, gran_bit = (row & s) != 0, (gran & s) != 0
        x = jnp.where(row_bit == gran_bit, x, jnp.where(gran_bit, down, up))
    return x


def kernel(
    patches_ref, region_ref, cell_ref, wf_ref, wd_ref, wp_ref, wm_ref, wo_ref,
    out_ref,
    gathered, slots_out, slots_in, sums_out, sums_in, sums_own, tables_out, tables_in, codes_out, codes_in,
    wf_raw, wd_raw, wp_raw, wm_raw, wo_raw,
    wf, wd, wp, wm, wo,
    select, place, grid_f, tile, halo, im1, im2, imd, im4, out_b,
    load, t_send, t_recv, c_send, c_recv, route_send, route_recv,
    w_send, w_recv, x_send, x_recv, h_send, h_recv, o_send, o_recv, o_own,
):
    r, c = lax.axis_index("region"), lax.axis_index("chan")
    at = (r // 16, (r // 4) % 4, r % 4)
    other = 1 - c

    def along(axis, step):
        z, y, x = ((at[a] + step) % 4 if a == axis else at[a] for a in range(3))
        return (z * 16 + y * 4 + x, c)

    def remote(src, dst, send, recv, device):
        return pltpu.make_async_remote_copy(
            src_ref=src, dst_ref=dst, send_sem=send, recv_sem=recv,
            device_id=device, device_id_type=MESH,
        )

    def greet(device):
        pl.semaphore_signal(barrier, inc=1, device_id=device, device_id_type=MESH)

    barrier = pltpu.get_barrier_semaphore()
    for axis in range(3):
        for step in STEPS:
            greet(along(axis, step))
    greet((r, other))

    encoder = [(wf_ref, wf_raw.at[c]), (wd_ref, wd_raw.at[c]), (wp_ref, wp_raw.at[c])]
    loads = [
        pltpu.make_async_copy(src, dst, load.at[n])
        for n, (src, dst) in enumerate(
            [(patches_ref, gathered.at[0])] + encoder + [(wm_ref, wm_raw), (wo_ref, wo_raw)]
        )
    ]
    for copy in loads:
        copy.start()

    earlier = (iota((64, 64), 0) < iota((64, 64), 1)).astype(F32).astype(BF16)
    before = jnp.zeros((64, 1), F32)
    entry = jnp.zeros((8, 64), F32)
    for t in range(2):
        target = region_ref[t : t + 1, :]
        hit = jnp.where(iota((64, 64), 0) == target, 1.0, 0.0)
        count = jnp.dot(hit.astype(BF16), earlier, preferred_element_type=F32) + before
        before = before + jnp.sum(hit, axis=1, keepdims=True)
        rank = jnp.sum(hit * count, axis=0, keepdims=True)
        entry = jnp.where(iota((8, 64), 0) == t, target.astype(F32) * 4.0 + rank, entry)
        entry = jnp.where(
            iota((8, 64), 0) == t + 2, cell_ref[t : t + 1, :].astype(F32), entry
        )
    twice = (iota((64, W), 1) % 64 == iota((64, W), 0)).astype(F32).astype(BF16)
    tables_out[...] = jnp.dot(entry.astype(BF16), twice, preferred_element_type=F32)

    chunks = jobs()
    loads[0].wait()
    pl.semaphore_wait(barrier, 10)
    for axis in range(3):
        for step in STEPS:
            remote(
                tables_out, tables_in.at[axis, step], t_send, t_recv.at[axis], along(axis, step)
            ).start()
        tables_in[axis, 0] = tables_out[...]

    def spread_out(phase, h, src, dst):
        for step in STEPS:
            for p, a, b in chunks[h]:
                lanes = pl.ds(a, b - a)
                remote(
                    src(step).at[:, lanes], dst.at[step, :, lanes],
                    route_send.at[phase], route_recv.at[phase, h, p],
                    along(PARTS[p][0][phase], step),
                ).start()

    def arrive(phase, h, p, a, b, dst):
        whole = dst.at[pl.ds(1, 3), :, pl.ds(a, b - a)]
        remote(whole, whole, route_send.at[phase], route_recv.at[phase, h, p], (r, other)).wait_recv()

    for h in range(3):
        spread_out(0, h, lambda step: gathered.at[0], gathered)

    weight_copies = [
        remote(src, dst, w_send.at[n], w_recv.at[n], (r, other)) for n, (src, dst) in enumerate(encoder)
    ]
    for copy in weight_copies:
        copy.start()
    for copy in loads[1:]:
        copy.wait()
    for copy in weight_copies:
        copy.wait_recv()
    taps_from = [k + other * (6 - 6 * (k // 3)) for k in range(9)]
    for core in range(2):
        wf[64 * core : 64 * core + 64, :] = jnp.concatenate(
            [wf_raw[core, k] for k in taps_from], axis=1
        )
    for k, source in enumerate(taps_from):
        i, j = k // 3, k % 3
        for core in range(2):
            wp[128 * core : 128 * core + 128, 256 * k : 256 * k + 256] = wp_raw[core, source]
        wm[:, 1152 * i + 128 * j : 1152 * i + 128 * j + 128] = wm_raw[source, :, :C1]
        wm[:, 1152 * i + 384 + 256 * j : 1152 * i + 384 + 256 * j + 256] = wm_raw[source, :, C1:]
        wo[:, 128 * k : 128 * k + 128] = wo_raw[source]

    for k in range(12):
        i, j = k // 3, k % 3
        source = 3 * (min(3 - i, 2) * other + min(i, 2) * c) + j
        used = (c == 1 if i == 0 else c == 0) if i in (0, 3) else None
        for core in range(2):
            value = wd_raw[core, source]
            if used is not None:
                value = jnp.where(used, value, jnp.zeros_like(value))
            wd[128 * core : 128 * core + 128, 128 * k : 128 * k + 128] = value

    lane = iota((8, W), 1)
    left = lane < 64
    for p, (axes, _) in enumerate(PARTS):
        here, second, third = axes
        three = tables_in.at[here, pl.ds(1, 3)]
        remote(three, three, t_send, t_recv.at[here], (r, other)).wait_recv()
        values = jnp.zeros((8, 256), F32)
        for half in range(2):
            table = jnp.where(left, tables_in[here, 2 * half], tables_in[here, 2 * half + 1])
            code = table.astype(jnp.int32)
            region = code // 4
            place_of = (region // 16, (region // 4) % 4, region % 4)
            slot = (
                ((place_of[second] - at[second]) & 3) * 64
                + (2 * half + lane // 64) * 16
                + ((place_of[third] - at[third]) & 3) * 4
                + code % 4
            )
            slot = jnp.where(place_of[here] == at[here], slot, -1)
            hits = [iota((256, W), 0) == slot[t : t + 1] for t in range(2)]
            select[p, :, W * half : W * half + W] = (
                jnp.where(jnp.logical_or(hits[0], hits[1]), 1.0, 0.0).astype(BF16)
            )
            for t in range(2):
                cells = jnp.broadcast_to(table[t + 2 : t + 3] + 1.0, (8, W)).astype(BF16)
                values = values + lax.dot_general(
                    cells, jnp.where(hits[t], 1.0, 0.0).astype(BF16),
                    (((1,), (1,)), ((), ())), preferred_element_type=F32,
                )
        for step in range(4):
            value = values[:, W * (step // 2) : W * (step // 2) + W]
            turned = pltpu.roll(value, 64, 1)
            value = jnp.where(left, value, turned) if step % 2 == 0 else jnp.where(left, turned, value)
            value = jnp.where(value > 0.0, value - 1.0 + (32 * ((lane // 4) % 4)).astype(F32), -1.0)
            if step == 0:
                codes_in[p, 0] = value
            else:
                codes_out[p, step] = value
        for step in STEPS:
            remote(
                codes_out.at[p, step], codes_in.at[p, step], c_send, c_recv.at[p], along(second, step)
            ).start()

    for h in range(3):
        for p, a, b in chunks[h]:
            arrive(0, h, p, a, b, gathered)
            for n in range(a, b, 256):
                e = min(n + 256, b)
                slots = jnp.dot(
                    select[p], gathered[:, :, n:e].reshape(256, e - n), preferred_element_type=F32
                ).astype(BF16)
                slots_in[0, :, n:e] = slots[:64]
                slots_out[:, :, n:e] = slots[64:].reshape(3, 64, e - n)
        spread_out(1, h, lambda step: slots_out.at[step - 1], slots_in)

    for p in range(3):
        three = codes_in.at[p, pl.ds(1, 3)]
        remote(three, three, c_send, c_recv.at[p], (r, other)).wait_recv()
        for half in range(2):
            code = jnp.where(left, codes_in[p, 2 * half], codes_in[p, 2 * half + 1])[0:1]
            place[p, :, W * half : W * half + W] = jnp.where(
                iota((W, W), 0).astype(F32) == code, 1.0, 0.0
            ).astype(BF16)
    for h in range(3):
        for p, a, b in chunks[h]:
            arrive(1, h, p, a, b, slots_in)
            for n in range(a, b, 256):
                e = min(n + 256, b)
                sums = jnp.dot(
                    place[p], slots_in[:, :, n:e].reshape(256, e - n), preferred_element_type=F32
                )
                sums_own[:, n:e] = sums[:32]
                sums_out[:, :, n:e] = sums[32:].astype(BF16).reshape(3, 32, e - n)
        spread_out(2, h, lambda step: sums_out.at[step - 1], sums_in)

    border = jnp.logical_or(jnp.logical_and(r == 0, c == 0), jnp.logical_and(r == 63, c == 1))
    keep = jnp.where(border, 0.0, 1.0)

    def tile_row(v):
        return (15 - v) * other + (16 + v) * c

    even = iota((C2, W), 1) % 2 == 0

    def taps(x):
        return shift(x, -1), x, shift(x, 1)

    def settle(e):
        mine = pl.ds(pl.multiple_of(32 * c + 16 * e, 16), 16)
        tile[:, mine, :] = grid_f[e].astype(BF16).reshape(32, 16, W)
        copy = remote(tile.at[:, mine], tile.at[:, mine], x_send.at[e], x_recv.at[e], (r, other))
        if e == 1:
            send_halo(e)
        copy.start()
        return copy

    def halo_copies(e, core):
        rows = pl.ds(pl.multiple_of(32 * core + 16 * e, 16), 16)
        for to in range(2):
            yield remote(
                tile.at[pl.ds(26 * (1 - to), 6), rows], halo.at[:, rows],
                h_send.at[e, to], h_recv.at[e, core], ((r + 1 + 62 * to) % 64, to),
            )

    def send_halo(e):
        for copy in halo_copies(e, c):
            copy.start()

    def widen(e, core):
        channels = pl.multiple_of(32 * core + 16 * e, 16)
        for l in range(22):
            for j, tap in enumerate(taps(tile[tile_row(l - 6), pl.ds(channels, 16), :])):
                im1[l, pl.ds(C0 * j + channels, 16), :] = tap

    tile_copies = []
    for h in range(3):
        for p, a, b in chunks[h]:
            arrive(2, h, p, a, b, sums_in)
            total = sums_own[:, a:b]
            for step in STEPS:
                total = total + sums_in[step, :, a:b].astype(F32)
            for n in range(a, b, W):
                block = swap_granules(total[:, n - a : n - a + W])
                e, ch = n // W // 16, n // W % 16
                for band in range(4):
                    grid_f[e, pl.ds(W * band + ch, 8, stride=16), :] = block[8 * band : 8 * band + 8]
        if h != 1:
            e = h // 2
            tile_copies.append(settle(e))
            widen(e, c)
            tile_copies[e].wait_recv()
            if e == 0:
                send_halo(e)
            widen(e, other)

    def first_rows_of(n):
        f = 4 * n
        window = jnp.concatenate(
            [im1[f + t : f + t + 3].reshape(576, W) for t in range(4)], axis=1
        )
        total = jnp.dot(wf[...], window, preferred_element_type=F32)
        for t in range(4):
            row = silu(total[:, W * t : W * t + W])
            if f + t >= 21:
                row = row * keep
            for j, tap in enumerate(taps(row.astype(BF16))):
                im2[f + t, C1 * j : C1 * j + C1] = tap

    def spread_pair(at_pair, x):
        for j, tap in enumerate((shift(x, -2), x, shift(x, 2))):
            imd[at_pair, C2 * j : C2 * j + C2] = tap

    def second_pair(m):
        window = jnp.concatenate(
            [
                jnp.concatenate([im2[4 * m + 2 * t + i, 0:384] for i in range(4)], axis=0)
                for t in range(2)
            ],
            axis=1,
        )
        total = jnp.dot(wd[...], window, preferred_element_type=F32)
        pair = silu(jnp.where(even, total[:, :W], pltpu.roll(total[:, W:], 1, 1)))
        if m == 5:
            pair = pair * keep
        spread_pair(2 * m, pair.astype(BF16))

    def blend(m):
        a, b = imd[2 * m, C2 : 2 * C2], imd[2 * m + 2, C2 : 2 * C2]
        spread_pair(2 * m + 1, jnp.where(even, shift(a, 1), shift(b, -1)))

    def third_pairs(ms):
        window = jnp.concatenate([imd[2 * m : 2 * m + 3].reshape(2304, W) for m in ms], axis=1)
        total = jnp.dot(wp[...], window, preferred_element_type=F32)
        for t, m in enumerate(ms):
            third = silu(total[:, W * t : W * t + W]) + imd[2 * m + 1, C2 : 2 * C2].astype(F32)
            if m == 4:
                third = jnp.where(even, third, third * keep)
            third = third.astype(BF16)
            l1, l2, r1, r2 = shift(third, -1), shift(third, -2), shift(third, 1), shift(third, 2)
            lane = iota((C2, W), 1)
            zero = jnp.zeros_like(third)
            ups = (
                (
                    jnp.where(even, l2, l1),
                    jnp.where(even, third, l1),
                    jnp.where(lane == W - 1, zero, jnp.where(even, third, r1)),
                ),
                (
                    jnp.where(lane == 0, zero, jnp.where(even, l1, third)),
                    jnp.where(even, r1, third),
                    jnp.where(even, r1, r2),
                ),
            )
            for half in range(2):
                for j in range(3):
                    f = 4 * m + 3 + 2 * half
                    im2[f, 384 + C2 * j : 384 + C2 * j + C2] = ups[half][j]
                    im2[f + 1, 384 + C2 * j : 384 + C2 * j + C2] = ups[half][j]

    def fourth_rows(n):
        g = 2 * n
        window = jnp.concatenate(
            [im2[g + 3 + t : g + 6 + t].reshape(3456, W) for t in range(2)], axis=1
        )
        total = jnp.dot(wm[...], window, preferred_element_type=F32)
        for t in range(2):
            row = silu(total[:, W * t : W * t + W])
            if g + t == 17:
                row = row * keep
            for j, tap in enumerate(taps(row.astype(BF16))):
                im4[g + t, C1 * j : C1 * j + C1] = tap

    def out_rows(n):
        f = 4 * n
        window = jnp.concatenate(
            [im4[f + t : f + t + 3].reshape(1152, W) for t in range(4)], axis=1
        )
        total = jnp.dot(wo[...], window, preferred_element_type=F32)
        for t in range(4):
            row = total[:, W * t : W * t + W] + tile[tile_row(f + t)].astype(F32)
            out_b[(15 - f - t) * other + (f + t) * c] = row.astype(BF16)
        start = (12 - f) * other + f * c
        source, target = out_b.at[pl.ds(start, 4)], out_ref.at[pl.ds(HALF * c + start, 4)]
        remote(
            source.at[:, pl.ds(pl.multiple_of(32 * other, 32), 32)], target, o_send, o_recv, (r, other)
        ).start()
        pltpu.make_async_copy(
            source.at[:, pl.ds(pl.multiple_of(32 * c, 32), 32)], target, o_own
        ).start()

    for n in range(5):
        first_rows_of(n)
        if n:
            second_pair(n - 1)
        if n > 1:
            blend(n - 2)
        if n == 3:
            third_pairs([0, 1])
    third_pairs([2])
    for n in range(3):
        fourth_rows(n)
    for e in range(2):
        for core in range(2):
            next(halo_copies(e, core)).wait_recv()

    @pl.when(border)
    def _():
        halo[...] = jnp.zeros((6, C0, W), BF16)

    for l in range(6):
        for j, tap in enumerate(taps(halo[(5 - l) * other + l * c])):
            im1[22 + l, C0 * j : C0 * j + C0] = tap
    for n in range(5, 7):
        first_rows_of(n)
    for m in range(4, 6):
        second_pair(m)
    for m in range(3, 5):
        blend(m)
    third_pairs([3, 4])
    for n in range(3, 9):
        fourth_rows(n)
    for n in range(4):
        out_rows(n)
    for copy in weight_copies + tile_copies + [*halo_copies(0, c), *halo_copies(1, c)]:
        copy.wait_send()
    for phase, buffer in enumerate((gathered, slots_in, sums_in)):
        whole = buffer.at[pl.ds(1, 3)]
        remote(whole, whole, route_send.at[phase], o_recv, (r, other)).wait_send()
    three = tables_in.at[:, pl.ds(1, 3)]
    remote(three, three, t_send, o_recv, (r, other)).wait_send()
    three = codes_in.at[:, pl.ds(1, 3)]
    remote(three, three, c_send, o_recv, (r, other)).wait_send()
    rows = out_ref.at[pl.ds(0, HALF)]
    remote(rows, rows, o_send, o_recv, (r, other)).wait()
    pltpu.make_async_copy(rows, rows, o_own).wait()


def shards(patches, region, cell, *weights):
    vmem = pl.BlockSpec(memory_space=pltpu.VMEM)
    anywhere = pl.BlockSpec(memory_space=pl.ANY)
    dma = pltpu.SemaphoreType.DMA
    rows = pl.pallas_call(
        kernel,
        out_shape=jax.ShapeDtypeStruct((32, 32, W), BF16),
        in_specs=[anywhere, vmem, vmem] + [anywhere] * 5,
        out_specs=anywhere,
        scratch_shapes=[
            pltpu.VMEM((4, 64, 4096), BF16),
            pltpu.VMEM((3, 64, 4096), BF16),
            pltpu.VMEM((4, 64, 4096), BF16),
            pltpu.VMEM((3, 32, 4096), BF16),
            pltpu.VMEM((4, 32, 4096), BF16),
            pltpu.VMEM((32, 4096), F32),
            pltpu.VMEM((8, W), F32),
            pltpu.VMEM((3, 4, 8, W), F32),
            pltpu.VMEM((3, 4, 8, W), F32),
            pltpu.VMEM((3, 4, 8, W), F32),
            pltpu.VMEM((2, 9, 64, C0), BF16),
            pltpu.VMEM((2, 9, 128, C1), BF16),
            pltpu.VMEM((2, 9, 128, C2), BF16),
            pltpu.VMEM((9, C1, C1 + C2), BF16),
            pltpu.VMEM((9, C0, C1), BF16),
            pltpu.VMEM((C1, 9 * C0), BF16),
            pltpu.VMEM((C2, 12 * C1), BF16),
            pltpu.VMEM((C2, 9 * C2), BF16),
            pltpu.VMEM((C1, 9 * (C1 + C2)), BF16),
            pltpu.VMEM((C0, 9 * C1), BF16),
            pltpu.VMEM((3, 256, 256), BF16),
            pltpu.VMEM((3, W, 256), BF16),
            pltpu.VMEM((2, 512, W), F32),
            pltpu.VMEM((32, C0, W), BF16),
            pltpu.VMEM((6, C0, W), BF16),
            pltpu.VMEM((30, 3 * C0, W), BF16),
            pltpu.VMEM((28, 3 * (C1 + C2), W), BF16),
            pltpu.VMEM((11, 3 * C2, W), BF16),
            pltpu.VMEM((18, 3 * C1, W), BF16),
            pltpu.VMEM((HALF, C0, W), BF16),
            dma((6,)), dma, dma((3,)), dma, dma((3,)), dma((3,)), dma((3, 3, 3)),
            dma((3,)), dma((3,)), dma((2,)), dma((2,)), dma((2, 2)), dma((2, 2)), dma, dma, dma,
        ],
        compiler_params=pltpu.CompilerParams(
            collective_id=0, has_side_effects=True, vmem_limit_bytes=56 << 20
        ),
    )(patches, region.T, cell.T, *weights)
    return jnp.transpose(rows, (1, 0, 2))


def solution(mesh):
    placed = (
        P("region", "chan"),
        P("region", None),
        P("region", None),
        P(None, "chan", None),
        P(None, "chan", None),
        P(None, "chan", None),
        P(),
        P(),
    )
    return jax.shard_map(
        shards, mesh=mesh, in_specs=placed, out_specs=P("chan", "region", None), check_vma=False
    )
```
